32 devices in a mesh: groups: 2 (over x), seq: 16 (over z, y, core).
Axes of the slice: x: 2, y: 2, z: 4, core: 2. Of those that a mesh axis runs over, the one named last changes fastest.
Arguments:
- qkv: bfloat16 [4096, 4096], P('seq', 'groups'), parts along dimension 1, may hold values from -6 to 6
- igate: float32 [4, 4096], P(None, ('groups', 'seq')), parts along dimension 1, may hold values from -110 to 100
- fgate: float32 [4, 4096], P(None, ('groups', 'seq')), parts along dimension 1, may hold values from 0 to 16
- doc_start: int32 [4096], P(('groups', 'seq')), parts along dimension 0, may hold values 0 or 1
- lengths: int32 [32], P(('groups', 'seq')), parts along dimension 0, may hold values from 1 to 128, 1536 in all
Outputs:
- mixed_out: bfloat16 [4096, 2048], P(('groups', 'seq')), parts along dimension 0
The draws below stay inside these ranges and needn't reach their ends.
There are 2 independent parts, one for each index of `groups`. The reference program is written for one: setup_inputs(seed, part) draws one part's arguments, and reference() takes and returns one part's arrays. A program takes and returns all parts, laid end to end along the dimension named above; each array names one. Nothing has to cross between parts.
Inputs may be any that keep to these rules, and one draw needn't show every extreme that they name: `lengths`: live positions of a shard come first, padding after them; the live counts of one sequence sum to 1536.
All inputs are finite; a program needn't handle non-finite values. No bound on the sum of `doc_start` on one device may be relied on, other than what follows from the above.
Results may differ from the reference program's by a relative error of at most 0.0056.
Values may be sent and summed in bfloat16 or wider, within the bound.
A program may use at most 128 MiB of HBM per device.

```python
import math
import jax
import jax.numpy as jnp
import numpy as np
from jax import lax

DK = 256
DV = 512
HEAD_COUNT_HALF = 4
TOK_DEV = 128
SEQUENCE_LENGTH = 2048
FEAT = 4096
SHARDS = 16


def draw_fgate(key, part):
    every_key_rows = jax.random.split(key, 5)
    blocks = SEQUENCE_LENGTH // TOK_DEV
    slow_share = 0.5
    slow_head = jax.random.uniform(every_key_rows[0], (HEAD_COUNT_HALF, 1)) < slow_share
    block_factor = jnp.repeat(jax.random.uniform(every_key_rows[1], (HEAD_COUNT_HALF, blocks), minval=0.3, maxval=1.0), TOK_DEV, axis=1)
    cell_factor = jax.random.uniform(every_key_rows[2], (HEAD_COUNT_HALF, SEQUENCE_LENGTH), minval=0.5, maxval=1.5)
    slow_rate = math.log(10.0) / (2.0 * SEQUENCE_LENGTH)
    forget_decay_speed = jnp.where(slow_head, slow_rate, 1.0 / 25.0) * block_factor * cell_factor
    spike_position = jax.random.randint(every_key_rows[3], (HEAD_COUNT_HALF, 2, 1), 0, SEQUENCE_LENGTH)
    token_position = jnp.arange(SEQUENCE_LENGTH)
    spike_flag = jnp.any(spike_position == token_position[None, None, :], axis=1)
    spike_penalty = jax.random.uniform(every_key_rows[4], (HEAD_COUNT_HALF, SEQUENCE_LENGTH), minval=0.22, maxval=0.69)
    forget_decay_speed = jnp.where(spike_flag, spike_penalty, forget_decay_speed)
    return (-jnp.log(jnp.expm1(forget_decay_speed))).astype(jnp.float32)


def draw_igate(key, part):
    every_key_rows = jax.random.split(jax.random.fold_in(key, 7), 1)
    base_values = jax.random.uniform(every_key_rows[0], (HEAD_COUNT_HALF, SEQUENCE_LENGTH), minval=-6.0, maxval=6.0)
    return base_values.astype(jnp.float32)


def touch_ends(entries, own_key, least, high):
    longest = entries.shape.index(max(entries.shape))
    spots = []
    for shift in (0, 1):
        where = [jax.random.randint(jax.random.fold_in(own_key, axis), (), 0, length) for axis, length in enumerate(entries.shape)]
        where[longest] = (where[longest] + shift) % entries.shape[longest]
        spots.append(tuple(where))
    return entries.at[spots[0]].set(least).at[spots[1]].set(high)


def block_scale(key, extent, cuts, low, high):
    loudness = 1.0
    for axis_at, shards_of in cuts:
        heights = jax.random.uniform(jax.random.fold_in(jax.random.fold_in(key, 6), axis_at), (shards_of,), jnp.float32, low / len(cuts), high / len(cuts))
        loudness = loudness * jnp.repeat(jnp.exp(heights), extent[axis_at] // shards_of).reshape((-1,) + (1,) * (len(extent) - 1 - axis_at))
    return loudness


def length_profile(count, total, bound, slope):
    loads = [(1 << 20) // math.isqrt(grade ** slope) + 1 for grade in range(2, count + 1)]
    spare, given = total - bound - (count - 1), [1] * (count - 1)
    while spare > 0:
        candidates = [i for i in range(count - 1) if given[i] < bound]
        pool, budget = sum([loads[i] for i in candidates]), spare
        for i in candidates:
            extra = min(bound - given[i], max(1, budget * loads[i] // pool), spare)
            given[i] = given[i] + extra
            spare = spare - extra
    return np.array([bound] + given)


def uneven(rng, amount, total, bound, lean):
    if amount == 2:
        one = jax.random.randint(rng, (), max(1, total - bound), min(bound, total - 1) + 1)
        return jnp.stack([one, total - one])
    tallies = jnp.asarray(length_profile(amount, total, bound, lean), jnp.int32)
    pairs = (amount - 1) // 2
    donor, sink = tallies[1:1 + 2 * pairs:2], tallies[2:2 + 2 * pairs:2]
    slack = jnp.minimum(donor - 1, bound - sink)
    moved = jax.random.randint(jax.random.fold_in(rng, 1), (pairs,), 0, 1 << 20) % (slack + 1)
    tallies = tallies.at[1:1 + 2 * pairs:2].set(donor - moved).at[2:2 + 2 * pairs:2].set(sink + moved)
    return tallies[jax.random.permutation(jax.random.fold_in(rng, 2), amount)]


def noise(key, shape, scale, bound, pieces=(), held_as=jnp.bfloat16):
    values = scale * jax.random.normal(key, shape, jnp.float32)
    if pieces:
        values = values * block_scale(key, shape, pieces, -0.22, 0.18)
    return jnp.clip(values, -bound, bound).astype(held_as)


def setup_inputs(seed: int = 0, part: int = 0) -> dict:
    key_list = jax.random.split(jax.random.key(seed), 6)
    part_keys = jax.random.split(jax.random.fold_in(key_list[5], part), 6)
    qkv = noise(part_keys[0], (FEAT, SEQUENCE_LENGTH), 1.0, 6.0, ((0, 16),))
    igate = draw_igate(jax.random.fold_in(jax.random.fold_in(key_list[5], part), 71), part)
    fgate = draw_fgate(jax.random.fold_in(jax.random.fold_in(key_list[5], part), 71), part)
    doc_start = touch_ends((jax.random.randint(part_keys[3], (SEQUENCE_LENGTH,), 0, 16 * TOK_DEV) < 1).astype(jnp.int32), jax.random.fold_in(part_keys[3], 1), 0, 1)
    lengths = uneven(part_keys[4], SHARDS, SEQUENCE_LENGTH * 3 // 4, TOK_DEV, 1).astype(jnp.int32)
    return dict(qkv=qkv, igate=igate, fgate=fgate, doc_start=doc_start, lengths=lengths)


empty_max = -1e+30
highest = lax.Precision.HIGHEST

def rounded(array):
    return lax.optimization_barrier(array.astype(jnp.bfloat16)).astype(jnp.float32)

def merge_states(earlier, later):
    early_state, early_normal, early_square, early_max, early_tail, early_open = earlier
    late_state, late_normal, late_square, late_max, late_tail, late_open = later
    passes = late_open > 0.5
    carried = late_tail + early_max
    largest = jnp.maximum(late_max, jnp.where(passes, carried, empty_max))
    keep_late = jnp.exp(late_max - largest)
    keep_early = jnp.where(passes, jnp.exp(carried - largest), 0.0)
    state = keep_late[:, None, None] * late_state + keep_early[:, None, None] * early_state
    normal = keep_late[:, None] * late_normal + keep_early[:, None] * early_normal
    square = keep_late * keep_late * late_square + keep_early * keep_early * early_square
    return (state, normal, square, largest, late_tail + early_tail, late_open * early_open)

def local_terms(queries, key_rows, value_rows, igate, fgate, doc_start, live_count):
    head_count, key_dim, width = queries.shape
    token_position = lax.iota(jnp.int32, width)
    living = token_position < live_count
    log_forget = jnp.where(living[None, :], jax.nn.log_sigmoid(fgate), 0.0)
    running = jnp.cumsum(log_forget, axis=1)
    resets = jnp.cumsum(doc_start, axis=0)
    allowed = (resets[:, None] == resets[None, :]) & (token_position[:, None] >= token_position[None, :]) & living[None, :]
    tail_doc = (resets == resets[width - 1]) & living
    key_scale = key_dim ** (-0.5)
    sums, denoms, squares, maxima = ([], [], [], [])
    states, normals, summary_sq, summary_max = ([], [], [], [])
    for head_index in range(head_count):
        exponent = running[head_index][:, None] - running[head_index][None, :] + igate[head_index][None, :]
        exponent = jnp.where(allowed, exponent, empty_max)
        row_max = lax.optimization_barrier(jnp.max(exponent, axis=1))
        weights = jnp.where(allowed, jnp.exp(exponent - row_max[:, None]), 0.0)
        scores = jnp.einsum('dt,ds->ts', queries[head_index], key_rows[head_index], precision=highest) * key_scale
        weighted = weights * scores
        sums.append(jnp.einsum('ts,js->tj', rounded(weighted), value_rows[head_index], precision=highest))
        denoms.append(lax.optimization_barrier(jnp.sum(weighted, axis=1)))
        squares.append(lax.optimization_barrier(jnp.sum(weights * weights, axis=1)))
        maxima.append(row_max)
        closing = running[head_index][width - 1] - running[head_index] + igate[head_index]
        closing = jnp.where(tail_doc, closing, empty_max)
        largest = jnp.max(closing)
        carried = jnp.where(tail_doc, jnp.exp(closing - largest), 0.0)
        scaled_keys = rounded(key_rows[head_index] * (carried * key_scale)[None, :])
        states.append(jnp.einsum('ds,js->dj', scaled_keys, value_rows[head_index], precision=highest))
        normals.append(lax.optimization_barrier(jnp.sum(scaled_keys, axis=1)))
        summary_sq.append(jnp.sum(carried * carried))
        summary_max.append(largest)
    open_flag = jnp.where(resets[width - 1] == 0, 1.0, 0.0).astype(jnp.float32).reshape(1)
    local_parts = (jnp.stack(sums, axis=1), jnp.stack(denoms, axis=1), jnp.stack(squares, axis=1), jnp.stack(maxima, axis=1), running.T, resets == 0, living)
    summary = (jnp.stack(states), jnp.stack(normals), jnp.stack(summary_sq), jnp.stack(summary_max), running[:, width - 1], open_flag)
    return (local_parts, summary)

def finish(local_parts, incoming, queries):
    sums, denoms, squares, maxima, running, first_open, living = local_parts
    state_in, normal_in, square_in, max_in = (incoming[0], incoming[1], incoming[2], incoming[3])
    incoming_exp = jnp.where(first_open[:, None], running + max_in[None, :], empty_max)
    largest = jnp.maximum(maxima, incoming_exp)
    own_scale = jnp.exp(maxima - largest)
    carry_scale = jnp.where(first_open[:, None], jnp.exp(incoming_exp - largest), 0.0)
    cross_term = jnp.einsum('hdt,hdj->thj', queries, rounded(state_in), precision=highest)
    cross_den = jnp.einsum('hdt,hd->th', queries, rounded(normal_in), precision=highest)
    numerator = own_scale[..., None] * sums + carry_scale[..., None] * cross_term
    denominator = own_scale * denoms + carry_scale * cross_den
    square = own_scale * own_scale * squares + carry_scale * carry_scale * square_in[None, :]
    divisor = jnp.where(living[:, None], jnp.maximum(jnp.abs(denominator), jnp.sqrt(square)), 1.0)
    result = jnp.where(living[:, None, None], numerator / divisor[..., None], 0.0)
    return result.reshape(result.shape[0], -1).astype(jnp.bfloat16)

def reference(qkv, igate, fgate, doc_start, lengths):
    blocks = SEQUENCE_LENGTH // TOK_DEV
    initial = (jnp.zeros((HEAD_COUNT_HALF, DK, DV), jnp.float32), jnp.zeros((HEAD_COUNT_HALF, DK), jnp.float32), jnp.zeros((HEAD_COUNT_HALF,), jnp.float32), jnp.full((HEAD_COUNT_HALF,), empty_max, jnp.float32), jnp.zeros((HEAD_COUNT_HALF,), jnp.float32), jnp.ones((1,), jnp.float32))

    def advance(carried_state, block_index):
        block_start = (block_index * TOK_DEV).astype(jnp.int32)
        block_rows = lax.dynamic_slice_in_dim(qkv, block_start, TOK_DEV, 1).astype(jnp.float32)
        queries = block_rows[:HEAD_COUNT_HALF * DK].reshape(HEAD_COUNT_HALF, DK, TOK_DEV)
        key_rows = block_rows[HEAD_COUNT_HALF * DK:2 * HEAD_COUNT_HALF * DK].reshape(HEAD_COUNT_HALF, DK, TOK_DEV)
        value_rows = block_rows[2 * HEAD_COUNT_HALF * DK:].reshape(HEAD_COUNT_HALF, DV, TOK_DEV)
        gate_in = lax.dynamic_slice_in_dim(igate, block_start, TOK_DEV, 1)
        gate_keep = lax.dynamic_slice_in_dim(fgate, block_start, TOK_DEV, 1)
        starts = lax.dynamic_slice_in_dim(doc_start, block_start, TOK_DEV, 0)
        live_count = lax.dynamic_index_in_dim(lengths, block_index, 0, keepdims=False)
        local_parts, summary = local_terms(queries, key_rows, value_rows, gate_in, gate_keep, starts, live_count)
        outputs = finish(local_parts, carried_state, queries)
        return (merge_states(carried_state, summary), outputs)
    final_state, outputs = lax.scan(advance, initial, jnp.arange(blocks, dtype=jnp.int32))
    return outputs.reshape(SEQUENCE_LENGTH, HEAD_COUNT_HALF * DV)
```

```python
import functools
import jax
import jax.numpy as jnp
from jax import lax
from jax.experimental import pallas as pl
from jax.experimental.pallas import tpu as pltpu
from jax.sharding import PartitionSpec as P

DK = 256
DV = 512
HEAD_COUNT_HALF = 4


empty_max = -1e30
highest = lax.Precision.HIGHEST


def running_sum(x):
    spots = lax.iota(jnp.int32, x.shape[-1])
    upto = spots[None, :] <= spots[:, None]
    return jnp.sum(jnp.where(upto, x[..., None, :], jnp.zeros((), x.dtype)), axis=-1)


def local_terms(queries, key_rows, value_rows, igate, fgate, doc_start, live_count):
    head_count, key_dim, width = queries.shape
    token_position = lax.iota(jnp.int32, width)
    living = token_position < live_count
    log_forget = jnp.where(living[None, :], jax.nn.log_sigmoid(fgate), 0.0)
    running = running_sum(log_forget)
    resets = running_sum(doc_start)
    allowed = (
        (resets[:, None] == resets[None, :])
        & (token_position[:, None] >= token_position[None, :])
        & living[None, :]
    )
    tail_doc = (resets == resets[width - 1]) & living
    key_scale = key_dim ** (-0.5)
    sums, denoms, squares, maxima = ([], [], [], [])
    states, normals, summary_sq, summary_max = ([], [], [], [])
    for head_index in range(head_count):
        exponent = (
            running[head_index][:, None] - running[head_index][None, :] + igate[head_index][None, :]
        )
        exponent = jnp.where(allowed, exponent, empty_max)
        row_max = jnp.max(exponent, axis=1)
        weights = jnp.where(allowed, jnp.exp(exponent - row_max[:, None]), 0.0)
        scores = (
            jnp.einsum(
                "dt,ds->ts",
                queries[head_index],
                key_rows[head_index],
                preferred_element_type=jnp.float32,
            )
            * key_scale
        )
        weighted = weights * scores
        sums.append(
            jnp.einsum(
                "ts,js->tj",
                weighted.astype(jnp.bfloat16),
                value_rows[head_index],
                preferred_element_type=jnp.float32,
            )
        )
        denoms.append(jnp.sum(weighted, axis=1))
        squares.append(jnp.sum(weights * weights, axis=1))
        maxima.append(row_max)
        closing = running[head_index][width - 1] - running[head_index] + igate[head_index]
        closing = jnp.where(tail_doc, closing, empty_max)
        largest = jnp.max(closing)
        carried = jnp.where(tail_doc, jnp.exp(closing - largest), 0.0)
        scaled_keys = (key_rows[head_index] * (carried * key_scale)[None, :]).astype(jnp.bfloat16)
        states.append(
            jnp.einsum(
                "ds,js->dj", scaled_keys, value_rows[head_index], preferred_element_type=jnp.float32
            )
        )
        normals.append(jnp.sum(scaled_keys.astype(jnp.float32), axis=1))
        summary_sq.append(jnp.sum(carried * carried))
        summary_max.append(largest)
    open_flag = jnp.where(resets[width - 1] == 0, 1.0, 0.0).astype(jnp.float32).reshape(1)
    local_parts = (
        jnp.stack(sums, axis=1),
        jnp.stack(denoms, axis=1),
        jnp.stack(squares, axis=1),
        jnp.stack(maxima, axis=1),
        running.T,
        resets == 0,
        living,
    )
    summary = (
        jnp.stack(states),
        jnp.stack(normals),
        jnp.stack(summary_sq),
        jnp.stack(summary_max),
        running[:, width - 1],
        open_flag,
    )
    return (local_parts, summary)


def finish(local_parts, incoming, queries):
    sums, denoms, squares, maxima, running, first_open, living = local_parts
    state_in, normal_in, square_in, max_in = (incoming[0], incoming[1], incoming[2], incoming[3])
    incoming_exp = jnp.where(first_open[:, None], running + max_in[None, :], empty_max)
    largest = jnp.maximum(maxima, incoming_exp)
    own_scale = jnp.exp(maxima - largest)
    carry_scale = jnp.where(first_open[:, None], jnp.exp(incoming_exp - largest), 0.0)
    cross_term = jnp.einsum(
        "hdt,hdj->thj", queries, state_in.astype(jnp.bfloat16), preferred_element_type=jnp.float32
    )
    cross_den = jnp.einsum(
        "hdt,hd->th", queries, normal_in.astype(jnp.bfloat16), preferred_element_type=jnp.float32
    )
    numerator = own_scale[..., None] * sums + carry_scale[..., None] * cross_term
    denominator = own_scale * denoms + carry_scale * cross_den
    square = own_scale * own_scale * squares + carry_scale * carry_scale * square_in[None, :]
    divisor = jnp.where(living[:, None], jnp.maximum(jnp.abs(denominator), jnp.sqrt(square)), 1.0)
    result = jnp.where(living[:, None, None], numerator / divisor[..., None], 0.0)
    return result.reshape(result.shape[0], -1).astype(jnp.bfloat16)


def spread_prefix(summary):
    states, normals, sq_sum, top_sum, tails, open_flag = summary
    shards = lax.axis_size("seq")
    own_index = lax.axis_index("seq")
    head_count, key_dim, value_dim = states.shape
    row_count = head_count * key_dim // shards
    spread = lax.all_to_all(
        states.reshape(1, head_count * key_dim, value_dim),
        "seq",
        split_axis=1,
        concat_axis=0,
        tiled=True,
    )
    normal_all, square_all, top_all, tail_all, open_all = (
        lax.all_gather(normals[None], "seq", axis=0, tiled=True),
        lax.all_gather(sq_sum[None], "seq", axis=0, tiled=True),
        lax.all_gather(top_sum[None], "seq", axis=0, tiled=True),
        lax.all_gather(tails[None], "seq", axis=0, tiled=True),
        lax.all_gather(open_flag, "seq", axis=0, tiled=True),
    )
    tails_after = running_sum(tail_all.T).T
    before = tails_after - tail_all
    closed_after = running_sum(1.0 - open_all)
    closed_before = closed_after - (1.0 - open_all)
    shard_order = lax.iota(jnp.int32, shards)
    linked = (shard_order[:, None] < shard_order[None, :]) & (
        closed_before[None, :] - closed_after[:, None] < 0.5
    )
    exponent = top_all[:, None, :] + before[None, :, :] - tails_after[:, None, :]
    exponent = jnp.where(linked[..., None], exponent, empty_max)
    entry_max = jnp.max(exponent, axis=0)
    weight = jnp.where(linked[..., None], jnp.exp(exponent - entry_max[None]), 0.0)
    own_pick = (shard_order == own_index).astype(jnp.float32)
    own_weight = jnp.einsum("ijh,j->ih", weight, own_pick, precision=highest)
    normal_in = jnp.einsum("ih,ihd->hd", own_weight, normal_all, precision=highest)
    square_in = jnp.einsum("ih,ih->h", own_weight * own_weight, square_all, precision=highest)
    max_in = jnp.einsum("jh,j->h", entry_max, own_pick, precision=highest)
    row_head = (own_index * row_count + lax.iota(jnp.int32, row_count)) // key_dim
    head_pick = (lax.iota(jnp.int32, head_count)[:, None] == row_head[None, :]).astype(jnp.float32)
    row_weight = jnp.einsum("ijh,hr->jir", weight, head_pick, precision=highest)
    state_rows = jnp.einsum("jir,irc->jrc", row_weight, spread, precision=highest)
    returned = lax.all_to_all(
        state_rows.astype(jnp.bfloat16), "seq", split_axis=0, concat_axis=1, tiled=True
    ).astype(state_rows.dtype)
    return (returned.reshape(head_count, key_dim, value_dim), normal_in, square_in, max_in)


def body(qkv, igate, fgate, doc_start, lengths):
    regrouped = lax.all_to_all(qkv, "seq", split_axis=1, concat_axis=0, tiled=True)
    width = igate.shape[1]
    queries = regrouped[: HEAD_COUNT_HALF * DK].reshape(HEAD_COUNT_HALF, DK, width)
    key_rows = regrouped[HEAD_COUNT_HALF * DK : 2 * HEAD_COUNT_HALF * DK].reshape(
        HEAD_COUNT_HALF, DK, width
    )
    value_rows = regrouped[2 * HEAD_COUNT_HALF * DK :].reshape(HEAD_COUNT_HALF, DV, width)
    local_parts, summary = local_terms(
        queries, key_rows, value_rows, igate, fgate, doc_start, lengths[0]
    )
    incoming = spread_prefix(summary)
    return finish(local_parts, incoming, queries)


MESH = pl.DeviceIdType.MESH
f32, bf16 = jnp.float32, jnp.bfloat16
HEADS = HEAD_COUNT_HALF
PARTS = DV // 128


def dot_nt(a, b):
    return lax.dot_general(a, b, (((1,), (1,)), ((), ())), preferred_element_type=f32)


def worker_kernel(
    qkv, ig, fg, doc, live_len, out,
    inbox, meta, metain, wts, qt, num, den, st_in, st_out, sm_in, sm_out, obuf,
    insend, inrecv, msend, mrecv, csend, crecv, osend, orecv,
):
    planes = HEADS
    width = ig.shape[1]
    span = planes * width
    g = lax.axis_index("groups")
    d = lax.axis_index("seq")
    p = lax.div(d, HEADS)
    h = lax.rem(d, HEADS)
    big = lax.div(d, 2 * HEADS)
    hd = (1 - big) * h + big * (lax.div(d, 2) - HEADS)
    role = (1 - big) * p + big * (2 + lax.rem(d, 2))
    peers = [lax.rem(h + i, HEADS) for i in range(1, HEADS)]

    pos = lax.broadcasted_iota(jnp.int32, (1, width), 1)
    live = pos < live_len[0]
    x = fg[...]
    a = jnp.where(live, jnp.minimum(x, 0.0) - jnp.log1p(jnp.exp(-jnp.abs(x))), 0.0)
    livef = jnp.where(live, 1.0, 0.0).astype(f32)
    docf = doc[...].astype(f32)
    pad = jnp.zeros((4, width), f32)
    for i in range(HEADS):
        meta[i] = jnp.concatenate([ig[i : i + 1, :], a[i : i + 1, :], docf, livef, pad], axis=0)

    bar = pltpu.get_barrier_semaphore()

    def greet(dev):
        pl.semaphore_signal(bar, inc=1, device_id=(g, dev), device_id_type=MESH)

    for s in (h, HEADS + h, 2 * HEADS + 2 * h, 2 * HEADS + 2 * h + 1):
        pl.when(s != d)(functools.partial(greet, s))
    for b in peers:
        greet(HEADS * p + b)
    pl.when(p > 0)(functools.partial(greet, d - HEADS))
    count = 2 * HEADS - 1 + jnp.where(p < planes - 1, 1, 0) - jnp.where(hd == h, 1, 0)
    pl.semaphore_wait(bar, count)

    def remote(src, dst, ss, rs, dev):
        return pltpu.make_async_remote_copy(
            src_ref=src, dst_ref=dst, send_sem=ss, recv_sem=rs, device_id=(g, dev), device_id_type=MESH
        )

    mcopies = [
        remote(meta.at[b], metain.at[h], msend.at[i], mrecv.at[h], HEADS * p + b)
        for i, b in enumerate(peers)
    ]
    for c in mcopies:
        c.start()
    metain[h] = meta[h]

    def feature(j):
        return remote(
            qkv.at[:, pl.ds(j * span, span)], inbox.at[role], insend.at[j], inrecv.at[role], HEADS * j + hd
        )

    for j in range(planes):
        away = HEADS * j + hd != d

        @pl.when(away)
        def _():
            feature(j).start()

        @pl.when(jnp.logical_not(away))
        def _():
            pltpu.make_async_copy(
                qkv.at[:, pl.ds(j * span, span)], inbox.at[role], inrecv.at[role]
            ).start()

    def landed(slot):
        pltpu.make_async_copy(inbox.at[slot], inbox.at[slot], inrecv.at[slot]).wait()

    for i, b in enumerate(peers):
        pltpu.make_async_copy(metain.at[b], metain.at[b], mrecv.at[b]).wait()

    rows = jnp.concatenate([metain[b] for b in range(planes)], axis=1)
    ig_row, a_row, doc_row, live_row = (rows[i : i + 1, :] for i in range(4))
    ti = lax.broadcasted_iota(jnp.int32, (span, span), 0)
    si = lax.broadcasted_iota(jnp.int32, (span, span), 1)
    tri = ti >= si
    eye = ti == si
    b_col = jnp.sum(jnp.where(tri, a_row, 0.0), axis=1, keepdims=True)
    r_col = jnp.sum(jnp.where(tri, doc_row, 0.0), axis=1, keepdims=True)
    live_col = jnp.sum(jnp.where(eye, live_row, 0.0), axis=1, keepdims=True)
    b_row = jnp.sum(jnp.where(eye, b_col, 0.0), axis=0, keepdims=True)
    r_row = jnp.sum(jnp.where(eye, r_col, 0.0), axis=0, keepdims=True)
    allowed = tri & (r_col == r_row) & (live_row > 0.5)
    ex = jnp.where(allowed, b_col - b_row + ig_row, empty_max)
    top = jnp.max(ex, axis=1, keepdims=True)
    weights = jnp.where(allowed, jnp.exp(ex - top), 0.0)
    wts[...] = weights
    sq_own = jnp.sum(weights * weights, axis=1, keepdims=True)
    b_end = b_row[:, span - 1 : span]
    r_end = r_row[:, span - 1 : span]
    tail = (r_row == r_end) & (live_row > 0.5)
    cl = jnp.where(tail, b_end - b_row + ig_row, empty_max)
    mu = jnp.max(cl, axis=1, keepdims=True)
    u = jnp.where(tail, jnp.exp(cl - mu), 0.0)
    sq_sum = jnp.sum(u * u, axis=1, keepdims=True)
    key_scale = DK ** (-0.5)

    def own():
        landed(0)
        qt[...] = inbox[0].astype(f32).T.astype(bf16)
        for b in range(planes):
            r = pl.ds(b * width, width)
            score = jnp.dot(qt[r, :], inbox[1], preferred_element_type=f32) * key_scale
            w = wts[r, :] * score
            den[r, :] = jnp.sum(w, axis=1, keepdims=True)
            wb = w.astype(bf16)
            for f in range(2):
                num[r, pl.ds(f * DK, DK)] = dot_nt(wb, inbox[2 + f])

    @pl.when(p == 0)
    def _():
        st_in[...] = jnp.zeros(st_in.shape, bf16)
        sm_in[...] = jnp.concatenate(
            [jnp.zeros((16, DK), f32), jnp.full((8, DK), empty_max, f32)], axis=0
        )

    landed(1)
    keyw = (inbox[1].astype(f32) * (u * key_scale)).astype(bf16)
    n8 = dot_nt(jnp.ones((8, span), bf16), keyw)
    landed(2)
    landed(3)
    pl.when(p >= 2)(own)

    sm_copy = remote(sm_out, sm_in, csend.at[PARTS], crecv.at[PARTS], d + HEADS)
    st_copies = [
        remote(st_out.at[c], st_in.at[c], csend.at[c], crecv.at[c], d + HEADS) for c in range(PARTS)
    ]

    @pl.when(p > 0)
    def _():
        pltpu.make_async_copy(sm_in, sm_in, crecv.at[PARTS]).wait()

    m_in = sm_in[16:17, 0:1]
    carried = b_end + m_in
    opened = r_end < 0.5
    largest = jnp.maximum(mu, jnp.where(opened, carried, empty_max))
    late = jnp.exp(mu - largest)
    early = jnp.where(opened, jnp.exp(carried - largest), 0.0)

    @pl.when(p < planes - 1)
    def _():
        sm_out[0:8, :] = late * n8 + early * sm_in[0:8, :]
        sm_out[8:16, :] = late * late * sq_sum + early * early * sm_in[8:16, :]
        sm_out[16:24, :] = jnp.broadcast_to(largest, (8, DK))
        sm_copy.start()

    for c in range(PARTS):

        @pl.when(p > 0)
        def _():
            pltpu.make_async_copy(st_in.at[c], st_in.at[c], crecv.at[c]).wait()

        @pl.when(p < planes - 1)
        def _():
            vals = inbox[2 + c // 2, pl.ds((c % 2) * 128, 128), :]
            st_out[c] = (late * dot_nt(keyw, vals) + early * st_in[c].astype(f32)).astype(bf16)
            st_copies[c].start()

    pl.when(p < 2)(own)

    nb = sm_in[0:8, :].astype(bf16)
    sq_in = sm_in[8:9, 0:1]

    def result(b):
        return remote(
            obuf.at[b], out.at[:, pl.ds(pl.multiple_of(h * DV, DV), DV)], osend.at[b], orecv.at[h], HEADS * p + b
        )

    def own_result(b):
        return pltpu.make_async_copy(
            obuf.at[b], out.at[:, pl.ds(pl.multiple_of(h * DV, DV), DV)], orecv.at[h]
        )

    for b in range(planes):
        lo, r = b * width, pl.ds(b * width, width)
        first = r_col[lo : lo + width] < 0.5
        f = jnp.where(first, b_col[lo : lo + width] + m_in, empty_max)
        mx = top[lo : lo + width]
        m = jnp.maximum(mx, f)
        xs = jnp.exp(mx - m)
        ys = jnp.where(first, jnp.exp(f - m), 0.0)
        qb = qt[r, :]
        dn = xs * den[r, :] + ys * dot_nt(qb, nb)[:, 0:1]
        sq = xs * xs * sq_own[lo : lo + width] + ys * ys * sq_in
        lv = live_col[lo : lo + width] > 0.5
        inv = 1.0 / jnp.where(lv, jnp.maximum(jnp.abs(dn), jnp.sqrt(sq)), 1.0)
        for c in range(PARTS):
            cs = pl.ds(c * 128, 128)
            cross = jnp.dot(qb, st_in[c], preferred_element_type=f32)
            obuf[b, :, cs] = jnp.where(lv, (xs * num[r, cs] + ys * cross) * inv, 0.0).astype(bf16)

        @pl.when(h != b)
        def _():
            result(b).start()

        @pl.when(h == b)
        def _():
            own_result(b).start()

    for i in range(HEADS):
        here = out.at[:, pl.ds(i * DV, DV)]
        pltpu.make_async_copy(here, here, orecv.at[i]).wait()
    for c in mcopies:
        c.wait_send()
    for j in range(planes):

        @pl.when(HEADS * j + hd != d)
        def _():
            feature(j).wait_send()

        @pl.when(h != j)
        def _():
            result(j).wait_send()

    @pl.when(p < planes - 1)
    def _():
        sm_copy.wait_send()
        for c in st_copies:
            c.wait_send()


def worker_body(qkv, igate, fgate, doc_start, lengths):
    width = igate.shape[1]
    span = HEADS * width
    vm = pl.BlockSpec(memory_space=pltpu.VMEM)
    dma = pltpu.SemaphoreType.DMA
    return pl.pallas_call(
        worker_kernel,
        out_shape=jax.ShapeDtypeStruct((width, HEADS * DV), bf16),
        in_specs=[pl.BlockSpec(memory_space=pl.ANY), vm, vm, vm, pl.BlockSpec(memory_space=pltpu.SMEM)],
        out_specs=pl.BlockSpec(memory_space=pl.ANY),
        scratch_shapes=[
            pltpu.VMEM((4, DK, span), bf16),
            pltpu.VMEM((HEADS, 8, width), f32),
            pltpu.VMEM((HEADS, 8, width), f32),
            pltpu.VMEM((span, span), f32),
            pltpu.VMEM((span, DK), bf16),
            pltpu.VMEM((span, DV), f32),
            pltpu.VMEM((span, 1), f32),
            pltpu.VMEM((PARTS, DK, 128), bf16),
            pltpu.VMEM((PARTS, DK, 128), bf16),
            pltpu.VMEM((24, DK), f32),
            pltpu.VMEM((24, DK), f32),
            pltpu.VMEM((HEADS, width, DV), bf16),
            dma((HEADS,)), dma((4,)), dma((HEADS - 1,)), dma((HEADS,)),
            dma((PARTS + 1,)), dma((PARTS + 1,)), dma((HEADS,)), dma((HEADS,)),
        ],
        compiler_params=pltpu.CompilerParams(
            collective_id=0, has_side_effects=True, vmem_limit_bytes=40 * 1024 * 1024
        ),
    )(qkv, igate, fgate, doc_start.reshape(1, width), lengths)


def solution(mesh):
    placed = (
        P("seq", "groups"),
        P(None, ("groups", "seq")),
        P(None, ("groups", "seq")),
        P(("groups", "seq")),
        P(("groups", "seq")),
    )
    shards = mesh.shape["seq"]
    whole_heads = shards == HEADS * HEADS and shards * DK == 2 * HEADS * DK + HEADS * DV
    return jax.shard_map(
        worker_body if whole_heads else body, mesh=mesh, in_specs=placed, out_specs=P(("groups", "seq"), None), check_vma=False
    )
```

```python
import functools
import jax
import jax.numpy as jnp
from jax import lax
from jax.experimental import pallas as pl
from jax.experimental.pallas import tpu as pltpu
from jax.sharding import PartitionSpec as P

DK = 256
DV = 512
HEAD_COUNT_HALF = 4


empty_max = -1e30
highest = lax.Precision.HIGHEST


def running_sum(x):
    spots = lax.iota(jnp.int32, x.shape[-1])
    upto = spots[None, :] <= spots[:, None]
    return jnp.sum(jnp.where(upto, x[..., None, :], jnp.zeros((), x.dtype)), axis=-1)


def local_terms(queries, key_rows, value_rows, igate, fgate, doc_start, live_count):
    head_count, key_dim, width = queries.shape
    token_position = lax.iota(jnp.int32, width)
    living = token_position < live_count
    log_forget = jnp.where(living[None, :], jax.nn.log_sigmoid(fgate), 0.0)
    running = running_sum(log_forget)
    resets = running_sum(doc_start)
    allowed = (
        (resets[:, None] == resets[None, :])
        & (token_position[:, None] >= token_position[None, :])
        & living[None, :]
    )
    tail_doc = (resets == resets[width - 1]) & living
    key_scale = key_dim ** (-0.5)
    sums, denoms, squares, maxima = ([], [], [], [])
    states, normals, summary_sq, summary_max = ([], [], [], [])
    for head_index in range(head_count):
        exponent = (
            running[head_index][:, None] - running[head_index][None, :] + igate[head_index][None, :]
        )
        exponent = jnp.where(allowed, exponent, empty_max)
        row_max = jnp.max(exponent, axis=1)
        weights = jnp.where(allowed, jnp.exp(exponent - row_max[:, None]), 0.0)
        scores = (
            jnp.einsum(
                "dt,ds->ts",
                queries[head_index],
                key_rows[head_index],
                preferred_element_type=jnp.float32,
            )
            * key_scale
        )
        weighted = weights * scores
        sums.append(
            jnp.einsum(
                "ts,js->tj",
                weighted.astype(jnp.bfloat16),
                value_rows[head_index],
                preferred_element_type=jnp.float32,
            )
        )
        denoms.append(jnp.sum(weighted, axis=1))
        squares.append(jnp.sum(weights * weights, axis=1))
        maxima.append(row_max)
        closing = running[head_index][width - 1] - running[head_index] + igate[head_index]
        closing = jnp.where(tail_doc, closing, empty_max)
        largest = jnp.max(closing)
        carried = jnp.where(tail_doc, jnp.exp(closing - largest), 0.0)
        scaled_keys = (key_rows[head_index] * (carried * key_scale)[None, :]).astype(jnp.bfloat16)
        states.append(
            jnp.einsum(
                "ds,js->dj", scaled_keys, value_rows[head_index], preferred_element_type=jnp.float32
            )
        )
        normals.append(jnp.sum(scaled_keys.astype(jnp.float32), axis=1))
        summary_sq.append(jnp.sum(carried * carried))
        summary_max.append(largest)
    open_flag = jnp.where(resets[width - 1] == 0, 1.0, 0.0).astype(jnp.float32).reshape(1)
    local_parts = (
        jnp.stack(sums, axis=1),
        jnp.stack(denoms, axis=1),
        jnp.stack(squares, axis=1),
        jnp.stack(maxima, axis=1),
        running.T,
        resets == 0,
        living,
    )
    summary = (
        jnp.stack(states),
        jnp.stack(normals),
        jnp.stack(summary_sq),
        jnp.stack(summary_max),
        running[:, width - 1],
        open_flag,
    )
    return (local_parts, summary)


def finish(local_parts, incoming, queries):
    sums, denoms, squares, maxima, running, first_open, living = local_parts
    state_in, normal_in, square_in, max_in = (incoming[0], incoming[1], incoming[2], incoming[3])
    incoming_exp = jnp.where(first_open[:, None], running + max_in[None, :], empty_max)
    largest = jnp.maximum(maxima, incoming_exp)
    own_scale = jnp.exp(maxima - largest)
    carry_scale = jnp.where(first_open[:, None], jnp.exp(incoming_exp - largest), 0.0)
    cross_term = jnp.einsum(
        "hdt,hdj->thj", queries, state_in.astype(jnp.bfloat16), preferred_element_type=jnp.float32
    )
    cross_den = jnp.einsum(
        "hdt,hd->th", queries, normal_in.astype(jnp.bfloat16), preferred_element_type=jnp.float32
    )
    numerator = own_scale[..., None] * sums + carry_scale[..., None] * cross_term
    denominator = own_scale * denoms + carry_scale * cross_den
    square = own_scale * own_scale * squares + carry_scale * carry_scale * square_in[None, :]
    divisor = jnp.where(living[:, None], jnp.maximum(jnp.abs(denominator), jnp.sqrt(square)), 1.0)
    result = jnp.where(living[:, None, None], numerator / divisor[..., None], 0.0)
    return result.reshape(result.shape[0], -1).astype(jnp.bfloat16)


def spread_prefix(summary):
    states, normals, sq_sum, top_sum, tails, open_flag = summary
    shards = lax.axis_size("seq")
    own_index = lax.axis_index("seq")
    head_count, key_dim, value_dim = states.shape
    row_count = head_count * key_dim // shards
    spread = lax.all_to_all(
        states.reshape(1, head_count * key_dim, value_dim),
        "seq",
        split_axis=1,
        concat_axis=0,
        tiled=True,
    )
    normal_all, square_all, top_all, tail_all, open_all = (
        lax.all_gather(normals[None], "seq", axis=0, tiled=True),
        lax.all_gather(sq_sum[None], "seq", axis=0, tiled=True),
        lax.all_gather(top_sum[None], "seq", axis=0, tiled=True),
        lax.all_gather(tails[None], "seq", axis=0, tiled=True),
        lax.all_gather(open_flag, "seq", axis=0, tiled=True),
    )
    tails_after = running_sum(tail_all.T).T
    before = tails_after - tail_all
    closed_after = running_sum(1.0 - open_all)
    closed_before = closed_after - (1.0 - open_all)
    shard_order = lax.iota(jnp.int32, shards)
    linked = (shard_order[:, None] < shard_order[None, :]) & (
        closed_before[None, :] - closed_after[:, None] < 0.5
    )
    exponent = top_all[:, None, :] + before[None, :, :] - tails_after[:, None, :]
    exponent = jnp.where(linked[..., None], exponent, empty_max)
    entry_max = jnp.max(exponent, axis=0)
    weight = jnp.where(linked[..., None], jnp.exp(exponent - entry_max[None]), 0.0)
    own_pick = (shard_order == own_index).astype(jnp.float32)
    own_weight = jnp.einsum("ijh,j->ih", weight, own_pick, precision=highest)
    normal_in = jnp.einsum("ih,ihd->hd", own_weight, normal_all, precision=highest)
    square_in = jnp.einsum("ih,ih->h", own_weight * own_weight, square_all, precision=highest)
    max_in = jnp.einsum("jh,j->h", entry_max, own_pick, precision=highest)
    row_head = (own_index * row_count + lax.iota(jnp.int32, row_count)) // key_dim
    head_pick = (lax.iota(jnp.int32, head_count)[:, None] == row_head[None, :]).astype(jnp.float32)
    row_weight = jnp.einsum("ijh,hr->jir", weight, head_pick, precision=highest)
    state_rows = jnp.einsum("jir,irc->jrc", row_weight, spread, precision=highest)
    returned = lax.all_to_all(
        state_rows.astype(jnp.bfloat16), "seq", split_axis=0, concat_axis=1, tiled=True
    ).astype(state_rows.dtype)
    return (returned.reshape(head_count, key_dim, value_dim), normal_in, square_in, max_in)


def body(qkv, igate, fgate, doc_start, lengths):
    regrouped = lax.all_to_all(qkv, "seq", split_axis=1, concat_axis=0, tiled=True)
    width = igate.shape[1]
    queries = regrouped[: HEAD_COUNT_HALF * DK].reshape(HEAD_COUNT_HALF, DK, width)
    key_rows = regrouped[HEAD_COUNT_HALF * DK : 2 * HEAD_COUNT_HALF * DK].reshape(
        HEAD_COUNT_HALF, DK, width
    )
    value_rows = regrouped[2 * HEAD_COUNT_HALF * DK :].reshape(HEAD_COUNT_HALF, DV, width)
    local_parts, summary = local_terms(
        queries, key_rows, value_rows, igate, fgate, doc_start, lengths[0]
    )
    incoming = spread_prefix(summary)
    return finish(local_parts, incoming, queries)


MESH = pl.DeviceIdType.MESH
f32, bf16 = jnp.float32, jnp.bfloat16
HEADS = HEAD_COUNT_HALF
PARTS = DV // 128


def dot_nt(a, b):
    return lax.dot_general(a, b, (((1,), (1,)), ((), ())), preferred_element_type=f32)


def worker_kernel(
    qkv, ig_hbm, fg_hbm, doc_hbm, live_len, out,
    ig, fg, doc, inbox, meta, metain, wts, qt, num, den, st_in, st_out, sm_in, sm_out, obuf,
    insend, inrecv, msend, mrecv, csend, crecv, osend, orecv, lsem,
):
    planes = HEADS
    width = ig_hbm.shape[1]
    span = planes * width
    g = lax.axis_index("groups")
    d = lax.axis_index("seq")
    p = lax.div(d, HEADS)
    h = lax.rem(d, HEADS)
    big = lax.div(d, 2 * HEADS)
    hd = (1 - big) * h + big * (lax.div(d, 2) - HEADS)
    role = (1 - big) * p + big * (2 + lax.rem(d, 2))
    peers = [lax.rem(h + i, HEADS) for i in range(1, HEADS)]

    loads = [
        pltpu.make_async_copy(src, dst, lsem.at[i])
        for i, (src, dst) in enumerate(((ig_hbm, ig), (fg_hbm, fg), (doc_hbm, doc)))
    ]
    for c in loads:
        c.start()

    bar = pltpu.get_barrier_semaphore()

    def greet(dev):
        pl.semaphore_signal(bar, inc=1, device_id=(g, dev), device_id_type=MESH)

    for s in (h, HEADS + h, 2 * HEADS + 2 * h, 2 * HEADS + 2 * h + 1):
        pl.when(s != d)(functools.partial(greet, s))
    for b in peers:
        greet(HEADS * p + b)
    pl.when(p > 0)(functools.partial(greet, d - HEADS))

    for c in loads:
        c.wait()
    pos = lax.broadcasted_iota(jnp.int32, (1, width), 1)
    live = pos < live_len[0]
    x = fg[...]
    a = jnp.where(live, jnp.minimum(x, 0.0) - jnp.log1p(jnp.exp(-jnp.abs(x))), 0.0)
    livef = jnp.where(live, 1.0, 0.0).astype(f32)
    docf = doc[...].astype(f32)
    pad = jnp.zeros((4, width), f32)
    for i in range(HEADS):
        meta[i] = jnp.concatenate([ig[i : i + 1, :], a[i : i + 1, :], docf, livef, pad], axis=0)

    count = 2 * HEADS - 1 + jnp.where(p < planes - 1, 1, 0) - jnp.where(hd == h, 1, 0)
    pl.semaphore_wait(bar, count)

    def remote(src, dst, ss, rs, dev):
        return pltpu.make_async_remote_copy(
            src_ref=src, dst_ref=dst, send_sem=ss, recv_sem=rs, device_id=(g, dev), device_id_type=MESH
        )

    mcopies = [
        remote(meta.at[b], metain.at[h], msend.at[i], mrecv.at[h], HEADS * p + b)
        for i, b in enumerate(peers)
    ]
    for c in mcopies:
        c.start()
    metain[h] = meta[h]

    def feature(j):
        return remote(
            qkv.at[:, pl.ds(j * span, span)], inbox.at[role], insend.at[j], inrecv.at[role], HEADS * j + hd
        )

    for j in range(planes):
        away = HEADS * j + hd != d

        @pl.when(away)
        def _():
            feature(j).start()

        @pl.when(jnp.logical_not(away))
        def _():
            pltpu.make_async_copy(
                qkv.at[:, pl.ds(j * span, span)], inbox.at[role], inrecv.at[role]
            ).start()

    def landed(slot):
        pltpu.make_async_copy(inbox.at[slot], inbox.at[slot], inrecv.at[slot]).wait()

    for i, b in enumerate(peers):
        pltpu.make_async_copy(metain.at[b], metain.at[b], mrecv.at[b]).wait()

    rows = jnp.concatenate([metain[b] for b in range(planes)], axis=1)
    ig_row, a_row, doc_row, live_row = (rows[i : i + 1, :] for i in range(4))
    ti = lax.broadcasted_iota(jnp.int32, (span, span), 0)
    si = lax.broadcasted_iota(jnp.int32, (span, span), 1)
    tri = ti >= si
    eye = ti == si
    b_col = jnp.sum(jnp.where(tri, a_row, 0.0), axis=1, keepdims=True)
    r_col = jnp.sum(jnp.where(tri, doc_row, 0.0), axis=1, keepdims=True)
    live_col = jnp.sum(jnp.where(eye, live_row, 0.0), axis=1, keepdims=True)
    b_row = jnp.sum(jnp.where(eye, b_col, 0.0), axis=0, keepdims=True)
    r_row = jnp.sum(jnp.where(eye, r_col, 0.0), axis=0, keepdims=True)
    allowed = tri & (r_col == r_row) & (live_row > 0.5)
    ex = jnp.where(allowed, b_col - b_row + ig_row, empty_max)
    top = jnp.max(ex, axis=1, keepdims=True)
    weights = jnp.where(allowed, jnp.exp(ex - top), 0.0)
    wts[...] = weights
    sq_own = jnp.sum(weights * weights, axis=1, keepdims=True)
    b_end = b_row[:, span - 1 : span]
    r_end = r_row[:, span - 1 : span]
    tail = (r_row == r_end) & (live_row > 0.5)
    cl = jnp.where(tail, b_end - b_row + ig_row, empty_max)
    mu = jnp.max(cl, axis=1, keepdims=True)
    u = jnp.where(tail, jnp.exp(cl - mu), 0.0)
    sq_sum = jnp.sum(u * u, axis=1, keepdims=True)
    key_scale = DK ** (-0.5)

    def own():
        landed(0)
        qt[...] = inbox[0].astype(f32).T.astype(bf16)
        for b in range(planes):
            r = pl.ds(b * width, width)
            score = jnp.dot(qt[r, :], inbox[1], preferred_element_type=f32) * key_scale
            w = wts[r, :] * score
            den[r, :] = jnp.sum(w, axis=1, keepdims=True)
            wb = w.astype(bf16)
            for f in range(2):
                num[r, pl.ds(f * DK, DK)] = dot_nt(wb, inbox[2 + f])

    @pl.when(p == 0)
    def _():
        st_in[...] = jnp.zeros(st_in.shape, bf16)
        sm_in[...] = jnp.concatenate(
            [jnp.zeros((16, DK), f32), jnp.full((8, DK), empty_max, f32)], axis=0
        )

    landed(1)
    keyw = (inbox[1].astype(f32) * (u * key_scale)).astype(bf16)
    n8 = dot_nt(jnp.ones((8, span), bf16), keyw)
    landed(2)
    landed(3)
    pl.when(p >= 2)(own)

    sm_copy = remote(sm_out, sm_in, csend.at[PARTS], crecv.at[PARTS], d + HEADS)
    st_copies = [
        remote(st_out.at[c], st_in.at[c], csend.at[c], crecv.at[c], d + HEADS) for c in range(PARTS)
    ]

    @pl.when(p > 0)
    def _():
        pltpu.make_async_copy(sm_in, sm_in, crecv.at[PARTS]).wait()

    m_in = sm_in[16:17, 0:1]
    carried = b_end + m_in
    opened = r_end < 0.5
    largest = jnp.maximum(mu, jnp.where(opened, carried, empty_max))
    late = jnp.exp(mu - largest)
    early = jnp.where(opened, jnp.exp(carried - largest), 0.0)

    @pl.when(p < planes - 1)
    def _():
        sm_out[0:8, :] = late * n8 + early * sm_in[0:8, :]
        sm_out[8:16, :] = late * late * sq_sum + early * early * sm_in[8:16, :]
        sm_out[16:24, :] = jnp.broadcast_to(largest, (8, DK))
        sm_copy.start()

    for c in range(PARTS):

        @pl.when(p > 0)
        def _():
            pltpu.make_async_copy(st_in.at[c], st_in.at[c], crecv.at[c]).wait()

        @pl.when(p < planes - 1)
        def _():
            vals = inbox[2 + c // 2, pl.ds((c % 2) * 128, 128), :]
            st_out[c] = (late * dot_nt(keyw, vals) + early * st_in[c].astype(f32)).astype(bf16)
            st_copies[c].start()

    pl.when(p < 2)(own)

    nb = sm_in[0:8, :].astype(bf16)
    sq_in = sm_in[8:9, 0:1]

    def result(b):
        return remote(
            obuf.at[b], out.at[:, pl.ds(pl.multiple_of(h * DV, DV), DV)], osend.at[b], orecv.at[h], HEADS * p + b
        )

    def own_result(b):
        return pltpu.make_async_copy(
            obuf.at[b], out.at[:, pl.ds(pl.multiple_of(h * DV, DV), DV)], orecv.at[h]
        )

    for b in range(planes):
        lo, r = b * width, pl.ds(b * width, width)
        first = r_col[lo : lo + width] < 0.5
        f = jnp.where(first, b_col[lo : lo + width] + m_in, empty_max)
        mx = top[lo : lo + width]
        m = jnp.maximum(mx, f)
        xs = jnp.exp(mx - m)
        ys = jnp.where(first, jnp.exp(f - m), 0.0)
        qb = qt[r, :]
        dn = xs * den[r, :] + ys * dot_nt(qb, nb)[:, 0:1]
        sq = xs * xs * sq_own[lo : lo + width] + ys * ys * sq_in
        lv = live_col[lo : lo + width] > 0.5
        inv = 1.0 / jnp.where(lv, jnp.maximum(jnp.abs(dn), jnp.sqrt(sq)), 1.0)
        for c in range(PARTS):
            cs = pl.ds(c * 128, 128)
            cross = jnp.dot(qb, st_in[c], preferred_element_type=f32)
            obuf[b, :, cs] = jnp.where(lv, (xs * num[r, cs] + ys * cross) * inv, 0.0).astype(bf16)

        @pl.when(h != b)
        def _():
            result(b).start()

        @pl.when(h == b)
        def _():
            own_result(b).start()

    for i in range(HEADS):
        here = out.at[:, pl.ds(i * DV, DV)]
        pltpu.make_async_copy(here, here, orecv.at[i]).wait()
    for c in mcopies:
        c.wait_send()
    for j in range(planes):

        @pl.when(HEADS * j + hd != d)
        def _():
            feature(j).wait_send()

        @pl.when(h != j)
        def _():
            result(j).wait_send()

    @pl.when(p < planes - 1)
    def _():
        sm_copy.wait_send()
        for c in st_copies:
            c.wait_send()


def worker_body(qkv, igate, fgate, doc_start, lengths):
    width = igate.shape[1]
    span = HEADS * width
    anywhere = pl.BlockSpec(memory_space=pl.ANY)
    dma = pltpu.SemaphoreType.DMA
    return pl.pallas_call(
        worker_kernel,
        out_shape=jax.ShapeDtypeStruct((width, HEADS * DV), bf16),
        in_specs=[anywhere] * 4 + [pl.BlockSpec(memory_space=pltpu.SMEM)],
        out_specs=pl.BlockSpec(memory_space=pl.ANY),
        scratch_shapes=[
            pltpu.VMEM((HEADS, width), f32),
            pltpu.VMEM((HEADS, width), f32),
            pltpu.VMEM((1, width), jnp.int32),
            pltpu.VMEM((4, DK, span), bf16),
            pltpu.VMEM((HEADS, 8, width), f32),
            pltpu.VMEM((HEADS, 8, width), f32),
            pltpu.VMEM((span, span), f32),
            pltpu.VMEM((span, DK), bf16),
            pltpu.VMEM((span, DV), f32),
            pltpu.VMEM((span, 1), f32),
            pltpu.VMEM((PARTS, DK, 128), bf16),
            pltpu.VMEM((PARTS, DK, 128), bf16),
            pltpu.VMEM((24, DK), f32),
            pltpu.VMEM((24, DK), f32),
            pltpu.VMEM((HEADS, width, DV), bf16),
            dma((HEADS,)), dma((4,)), dma((HEADS - 1,)), dma((HEADS,)),
            dma((PARTS + 1,)), dma((PARTS + 1,)), dma((HEADS,)), dma((HEADS,)), dma((3,)),
        ],
        compiler_params=pltpu.CompilerParams(
            collective_id=0, has_side_effects=True, vmem_limit_bytes=60 * 1024 * 1024
        ),
    )(qkv, igate, fgate, doc_start.reshape(1, width), lengths)


def solution(mesh):
    placed = (
        P("seq", "groups"),
        P(None, ("groups", "seq")),
        P(None, ("groups", "seq")),
        P(("groups", "seq")),
        P(("groups", "seq")),
    )
    shards = mesh.shape["seq"]
    whole_heads = shards == HEADS * HEADS and shards * DK == 2 * HEADS * DK + HEADS * DV
    return jax.shard_map(
        worker_body if whole_heads else body, mesh=mesh, in_specs=placed, out_specs=P(("groups", "seq"), None), check_vma=False
    )
```

```python
import functools
import jax
import jax.numpy as jnp
from jax import lax
from jax.experimental import pallas as pl
from jax.experimental.pallas import tpu as pltpu
from jax.sharding import PartitionSpec as P

DK = 256
DV = 512
HEAD_COUNT_HALF = 4


empty_max = -1e30
highest = lax.Precision.HIGHEST


def running_sum(x):
    spots = lax.iota(jnp.int32, x.shape[-1])
    upto = spots[None, :] <= spots[:, None]
    return jnp.sum(jnp.where(upto, x[..., None, :], jnp.zeros((), x.dtype)), axis=-1)


def local_terms(queries, key_rows, value_rows, igate, fgate, doc_start, live_count):
    head_count, key_dim, width = queries.shape
    token_position = lax.iota(jnp.int32, width)
    living = token_position < live_count
    log_forget = jnp.where(living[None, :], jax.nn.log_sigmoid(fgate), 0.0)
    running = running_sum(log_forget)
    resets = running_sum(doc_start)
    allowed = (
        (resets[:, None] == resets[None, :])
        & (token_position[:, None] >= token_position[None, :])
        & living[None, :]
    )
    tail_doc = (resets == resets[width - 1]) & living
    key_scale = key_dim ** (-0.5)
    sums, denoms, squares, maxima = ([], [], [], [])
    states, normals, summary_sq, summary_max = ([], [], [], [])
    for head_index in range(head_count):
        exponent = (
            running[head_index][:, None] - running[head_index][None, :] + igate[head_index][None, :]
        )
        exponent = jnp.where(allowed, exponent, empty_max)
        row_max = jnp.max(exponent, axis=1)
        weights = jnp.where(allowed, jnp.exp(exponent - row_max[:, None]), 0.0)
        scores = (
            jnp.einsum(
                "dt,ds->ts",
                queries[head_index],
                key_rows[head_index],
                preferred_element_type=jnp.float32,
            )
            * key_scale
        )
        weighted = weights * scores
        sums.append(
            jnp.einsum(
                "ts,js->tj",
                weighted.astype(jnp.bfloat16),
                value_rows[head_index],
                preferred_element_type=jnp.float32,
            )
        )
        denoms.append(jnp.sum(weighted, axis=1))
        squares.append(jnp.sum(weights * weights, axis=1))
        maxima.append(row_max)
        closing = running[head_index][width - 1] - running[head_index] + igate[head_index]
        closing = jnp.where(tail_doc, closing, empty_max)
        largest = jnp.max(closing)
        carried = jnp.where(tail_doc, jnp.exp(closing - largest), 0.0)
        scaled_keys = (key_rows[head_index] * (carried * key_scale)[None, :]).astype(jnp.bfloat16)
        states.append(
            jnp.einsum(
                "ds,js->dj", scaled_keys, value_rows[head_index], preferred_element_type=jnp.float32
            )
        )
        normals.append(jnp.sum(scaled_keys.astype(jnp.float32), axis=1))
        summary_sq.append(jnp.sum(carried * carried))
        summary_max.append(largest)
    open_flag = jnp.where(resets[width - 1] == 0, 1.0, 0.0).astype(jnp.float32).reshape(1)
    local_parts = (
        jnp.stack(sums, axis=1),
        jnp.stack(denoms, axis=1),
        jnp.stack(squares, axis=1),
        jnp.stack(maxima, axis=1),
        running.T,
        resets == 0,
        living,
    )
    summary = (
        jnp.stack(states),
        jnp.stack(normals),
        jnp.stack(summary_sq),
        jnp.stack(summary_max),
        running[:, width - 1],
        open_flag,
    )
    return (local_parts, summary)


def finish(local_parts, incoming, queries):
    sums, denoms, squares, maxima, running, first_open, living = local_parts
    state_in, normal_in, square_in, max_in = (incoming[0], incoming[1], incoming[2], incoming[3])
    incoming_exp = jnp.where(first_open[:, None], running + max_in[None, :], empty_max)
    largest = jnp.maximum(maxima, incoming_exp)
    own_scale = jnp.exp(maxima - largest)
    carry_scale = jnp.where(first_open[:, None], jnp.exp(incoming_exp - largest), 0.0)
    cross_term = jnp.einsum(
        "hdt,hdj->thj", queries, state_in.astype(jnp.bfloat16), preferred_element_type=jnp.float32
    )
    cross_den = jnp.einsum(
        "hdt,hd->th", queries, normal_in.astype(jnp.bfloat16), preferred_element_type=jnp.float32
    )
    numerator = own_scale[..., None] * sums + carry_scale[..., None] * cross_term
    denominator = own_scale * denoms + carry_scale * cross_den
    square = own_scale * own_scale * squares + carry_scale * carry_scale * square_in[None, :]
    divisor = jnp.where(living[:, None], jnp.maximum(jnp.abs(denominator), jnp.sqrt(square)), 1.0)
    result = jnp.where(living[:, None, None], numerator / divisor[..., None], 0.0)
    return result.reshape(result.shape[0], -1).astype(jnp.bfloat16)


def spread_prefix(summary):
    states, normals, sq_sum, top_sum, tails, open_flag = summary
    shards = lax.axis_size("seq")
    own_index = lax.axis_index("seq")
    head_count, key_dim, value_dim = states.shape
    row_count = head_count * key_dim // shards
    spread = lax.all_to_all(
        states.reshape(1, head_count * key_dim, value_dim),
        "seq",
        split_axis=1,
        concat_axis=0,
        tiled=True,
    )
    normal_all, square_all, top_all, tail_all, open_all = (
        lax.all_gather(normals[None], "seq", axis=0, tiled=True),
        lax.all_gather(sq_sum[None], "seq", axis=0, tiled=True),
        lax.all_gather(top_sum[None], "seq", axis=0, tiled=True),
        lax.all_gather(tails[None], "seq", axis=0, tiled=True),
        lax.all_gather(open_flag, "seq", axis=0, tiled=True),
    )
    tails_after = running_sum(tail_all.T).T
    before = tails_after - tail_all
    closed_after = running_sum(1.0 - open_all)
    closed_before = closed_after - (1.0 - open_all)
    shard_order = lax.iota(jnp.int32, shards)
    linked = (shard_order[:, None] < shard_order[None, :]) & (
        closed_before[None, :] - closed_after[:, None] < 0.5
    )
    exponent = top_all[:, None, :] + before[None, :, :] - tails_after[:, None, :]
    exponent = jnp.where(linked[..., None], exponent, empty_max)
    entry_max = jnp.max(exponent, axis=0)
    weight = jnp.where(linked[..., None], jnp.exp(exponent - entry_max[None]), 0.0)
    own_pick = (shard_order == own_index).astype(jnp.float32)
    own_weight = jnp.einsum("ijh,j->ih", weight, own_pick, precision=highest)
    normal_in = jnp.einsum("ih,ihd->hd", own_weight, normal_all, precision=highest)
    square_in = jnp.einsum("ih,ih->h", own_weight * own_weight, square_all, precision=highest)
    max_in = jnp.einsum("jh,j->h", entry_max, own_pick, precision=highest)
    row_head = (own_index * row_count + lax.iota(jnp.int32, row_count)) // key_dim
    head_pick = (lax.iota(jnp.int32, head_count)[:, None] == row_head[None, :]).astype(jnp.float32)
    row_weight = jnp.einsum("ijh,hr->jir", weight, head_pick, precision=highest)
    state_rows = jnp.einsum("jir,irc->jrc", row_weight, spread, precision=highest)
    returned = lax.all_to_all(
        state_rows.astype(jnp.bfloat16), "seq", split_axis=0, concat_axis=1, tiled=True
    ).astype(state_rows.dtype)
    return (returned.reshape(head_count, key_dim, value_dim), normal_in, square_in, max_in)


def body(qkv, igate, fgate, doc_start, lengths):
    regrouped = lax.all_to_all(qkv, "seq", split_axis=1, concat_axis=0, tiled=True)
    width = igate.shape[1]
    queries = regrouped[: HEAD_COUNT_HALF * DK].reshape(HEAD_COUNT_HALF, DK, width)
    key_rows = regrouped[HEAD_COUNT_HALF * DK : 2 * HEAD_COUNT_HALF * DK].reshape(
        HEAD_COUNT_HALF, DK, width
    )
    value_rows = regrouped[2 * HEAD_COUNT_HALF * DK :].reshape(HEAD_COUNT_HALF, DV, width)
    local_parts, summary = local_terms(
        queries, key_rows, value_rows, igate, fgate, doc_start, lengths[0]
    )
    incoming = spread_prefix(summary)
    return finish(local_parts, incoming, queries)


MESH = pl.DeviceIdType.MESH
f32, bf16 = jnp.float32, jnp.bfloat16
HEADS = HEAD_COUNT_HALF
PARTS = DV // 128


def dot_nt(a, b):
    return lax.dot_general(a, b, (((1,), (1,)), ((), ())), preferred_element_type=f32)


def worker_kernel(
    qkv, ig_hbm, fg_hbm, doc_hbm, live_len, out,
    ig, fg, doc, inbox, meta, metain, wts, qt, num, den, st_in, st_out, sm_in, sm_out, obuf,
    insend, inrecv, msend, mrecv, csend, crecv, osend, orecv, lsem,
):
    planes = HEADS
    width = ig_hbm.shape[1]
    span = planes * width
    g = lax.axis_index("groups")
    d = lax.axis_index("seq")
    p = lax.div(d, HEADS)
    h = lax.rem(d, HEADS)
    big = lax.div(d, 2 * HEADS)
    hd = (1 - big) * h + big * (lax.div(d, 2) - HEADS)
    role = (1 - big) * p + big * (2 + lax.rem(d, 2))
    peers = [lax.rem(h + i, HEADS) for i in range(1, HEADS)]

    loads = [
        pltpu.make_async_copy(src, dst, lsem.at[i])
        for i, (src, dst) in enumerate(((ig_hbm, ig), (fg_hbm, fg), (doc_hbm, doc)))
    ]
    for c in loads:
        c.start()

    bar = pltpu.get_barrier_semaphore()

    def greet(dev):
        pl.semaphore_signal(bar, inc=1, device_id=(g, dev), device_id_type=MESH)

    for s in (h, HEADS + h, 2 * HEADS + 2 * h, 2 * HEADS + 2 * h + 1):
        pl.when(s != d)(functools.partial(greet, s))
    for b in peers:
        greet(HEADS * p + b)
    pl.when(p > 0)(functools.partial(greet, d - HEADS))

    for c in loads:
        c.wait()
    pos = lax.broadcasted_iota(jnp.int32, (1, width), 1)
    live = pos < live_len[0]
    x = fg[...]
    a = jnp.where(live, jnp.minimum(x, 0.0) - jnp.log1p(jnp.exp(-jnp.abs(x))), 0.0)
    livef = jnp.where(live, 1.0, 0.0).astype(f32)
    docf = doc[...].astype(f32)
    pad = jnp.zeros((4, width), f32)
    for i in range(HEADS):
        meta[i] = jnp.concatenate([ig[i : i + 1, :], a[i : i + 1, :], docf, livef, pad], axis=0)

    count = 2 * HEADS - 1 + jnp.where(p < planes - 1, 1, 0) - jnp.where(hd == h, 1, 0)
    pl.semaphore_wait(bar, count)

    def remote(src, dst, ss, rs, dev):
        return pltpu.make_async_remote_copy(
            src_ref=src, dst_ref=dst, send_sem=ss, recv_sem=rs, device_id=(g, dev), device_id_type=MESH
        )

    mcopies = [
        remote(meta.at[b], metain.at[h], msend.at[i], mrecv.at[h], HEADS * p + b)
        for i, b in enumerate(peers)
    ]
    for c in mcopies:
        c.start()
    metain[h] = meta[h]

    def feature(j):
        return remote(
            qkv.at[:, pl.ds(j * span, span)], inbox.at[role], insend.at[j], inrecv.at[role], HEADS * j + hd
        )

    def send(j):
        away = HEADS * j + hd != d

        @pl.when(away)
        def _():
            feature(j).start()

        @pl.when(jnp.logical_not(away))
        def _():
            pltpu.make_async_copy(
                qkv.at[:, pl.ds(j * span, span)], inbox.at[role], inrecv.at[role]
            ).start()

    def send_rest():
        for j in range(1, planes):
            send(j)

    send(0)
    pl.when(big == 0)(send_rest)

    def landed(slot):
        pltpu.make_async_copy(inbox.at[slot], inbox.at[slot], inrecv.at[slot]).wait()

    for i, b in enumerate(peers):
        pltpu.make_async_copy(metain.at[b], metain.at[b], mrecv.at[b]).wait()

    rows = jnp.concatenate([metain[b] for b in range(planes)], axis=1)
    ig_row, a_row, doc_row, live_row = (rows[i : i + 1, :] for i in range(4))
    ti = lax.broadcasted_iota(jnp.int32, (span, span), 0)
    si = lax.broadcasted_iota(jnp.int32, (span, span), 1)
    tri = ti >= si
    eye = ti == si
    b_col = jnp.sum(jnp.where(tri, a_row, 0.0), axis=1, keepdims=True)
    r_col = jnp.sum(jnp.where(tri, doc_row, 0.0), axis=1, keepdims=True)
    live_col = jnp.sum(jnp.where(eye, live_row, 0.0), axis=1, keepdims=True)
    b_row = jnp.sum(jnp.where(eye, b_col, 0.0), axis=0, keepdims=True)
    r_row = jnp.sum(jnp.where(eye, r_col, 0.0), axis=0, keepdims=True)
    allowed = tri & (r_col == r_row) & (live_row > 0.5)
    ex = jnp.where(allowed, b_col - b_row + ig_row, empty_max)
    top = jnp.max(ex, axis=1, keepdims=True)
    weights = jnp.where(allowed, jnp.exp(ex - top), 0.0)
    wts[...] = weights
    sq_own = jnp.sum(weights * weights, axis=1, keepdims=True)
    b_end = b_row[:, span - 1 : span]
    r_end = r_row[:, span - 1 : span]
    tail = (r_row == r_end) & (live_row > 0.5)
    cl = jnp.where(tail, b_end - b_row + ig_row, empty_max)
    mu = jnp.max(cl, axis=1, keepdims=True)
    u = jnp.where(tail, jnp.exp(cl - mu), 0.0)
    sq_sum = jnp.sum(u * u, axis=1, keepdims=True)
    key_scale = DK ** (-0.5)
    pl.when(big > 0)(send_rest)

    def own():
        landed(0)
        qt[...] = inbox[0].astype(f32).T.astype(bf16)
        for b in range(planes):
            r = pl.ds(b * width, width)
            score = jnp.dot(qt[r, :], inbox[1], preferred_element_type=f32) * key_scale
            w = wts[r, :] * score
            den[r, :] = jnp.sum(w, axis=1, keepdims=True)
            wb = w.astype(bf16)
            for f in range(2):
                num[r, pl.ds(f * DK, DK)] = dot_nt(wb, inbox[2 + f])

    @pl.when(p == 0)
    def _():
        st_in[...] = jnp.zeros(st_in.shape, bf16)
        sm_in[...] = jnp.concatenate(
            [jnp.zeros((16, DK), f32), jnp.full((8, DK), empty_max, f32)], axis=0
        )

    landed(1)
    keyw = (inbox[1].astype(f32) * (u * key_scale)).astype(bf16)
    n8 = dot_nt(jnp.ones((8, span), bf16), keyw)
    landed(2)
    landed(3)
    pl.when(p >= 2)(own)

    sm_copy = remote(sm_out, sm_in, csend.at[PARTS], crecv.at[PARTS], d + HEADS)
    st_copies = [
        remote(st_out.at[c], st_in.at[c], csend.at[c], crecv.at[c], d + HEADS) for c in range(PARTS)
    ]

    @pl.when(p > 0)
    def _():
        pltpu.make_async_copy(sm_in, sm_in, crecv.at[PARTS]).wait()

    m_in = sm_in[16:17, 0:1]
    carried = b_end + m_in
    opened = r_end < 0.5
    largest = jnp.maximum(mu, jnp.where(opened, carried, empty_max))
    late = jnp.exp(mu - largest)
    early = jnp.where(opened, jnp.exp(carried - largest), 0.0)

    @pl.when(p < planes - 1)
    def _():
        sm_out[0:8, :] = late * n8 + early * sm_in[0:8, :]
        sm_out[8:16, :] = late * late * sq_sum + early * early * sm_in[8:16, :]
        sm_out[16:24, :] = jnp.broadcast_to(largest, (8, DK))
        sm_copy.start()

    for c in range(PARTS):

        @pl.when(p > 0)
        def _():
            pltpu.make_async_copy(st_in.at[c], st_in.at[c], crecv.at[c]).wait()

        @pl.when(p < planes - 1)
        def _():
            vals = inbox[2 + c // 2, pl.ds((c % 2) * 128, 128), :]
            st_out[c] = (late * dot_nt(keyw, vals) + early * st_in[c].astype(f32)).astype(bf16)
            st_copies[c].start()

    pl.when(p < 2)(own)

    nb = sm_in[0:8, :].astype(bf16)
    sq_in = sm_in[8:9, 0:1]

    def result(b):
        return remote(
            obuf.at[b], out.at[:, pl.ds(pl.multiple_of(h * DV, DV), DV)], osend.at[b], orecv.at[h], HEADS * p + b
        )

    def own_result(b):
        return pltpu.make_async_copy(
            obuf.at[b], out.at[:, pl.ds(pl.multiple_of(h * DV, DV), DV)], orecv.at[h]
        )

    for b in range(planes):
        lo, r = b * width, pl.ds(b * width, width)
        first = r_col[lo : lo + width] < 0.5
        f = jnp.where(first, b_col[lo : lo + width] + m_in, empty_max)
        mx = top[lo : lo + width]
        m = jnp.maximum(mx, f)
        xs = jnp.exp(mx - m)
        ys = jnp.where(first, jnp.exp(f - m), 0.0)
        qb = qt[r, :]
        dn = xs * den[r, :] + ys * dot_nt(qb, nb)[:, 0:1]
        sq = xs * xs * sq_own[lo : lo + width] + ys * ys * sq_in
        lv = live_col[lo : lo + width] > 0.5
        inv = 1.0 / jnp.where(lv, jnp.maximum(jnp.abs(dn), jnp.sqrt(sq)), 1.0)
        for c in range(PARTS):
            cs = pl.ds(c * 128, 128)
            cross = jnp.dot(qb, st_in[c], preferred_element_type=f32)
            obuf[b, :, cs] = jnp.where(lv, (xs * num[r, cs] + ys * cross) * inv, 0.0).astype(bf16)

        @pl.when(h != b)
        def _():
            result(b).start()

        @pl.when(h == b)
        def _():
            own_result(b).start()

    for i in range(HEADS):
        here = out.at[:, pl.ds(i * DV, DV)]
        pltpu.make_async_copy(here, here, orecv.at[i]).wait()
    for c in mcopies:
        c.wait_send()
    for j in range(planes):

        @pl.when(HEADS * j + hd != d)
        def _():
            feature(j).wait_send()

        @pl.when(h != j)
        def _():
            result(j).wait_send()

    @pl.when(p < planes - 1)
    def _():
        sm_copy.wait_send()
        for c in st_copies:
            c.wait_send()


def worker_body(qkv, igate, fgate, doc_start, lengths):
    width = igate.shape[1]
    span = HEADS * width
    anywhere = pl.BlockSpec(memory_space=pl.ANY)
    dma = pltpu.SemaphoreType.DMA
    return pl.pallas_call(
        worker_kernel,
        out_shape=jax.ShapeDtypeStruct((width, HEADS * DV), bf16),
        in_specs=[anywhere] * 4 + [pl.BlockSpec(memory_space=pltpu.SMEM)],
        out_specs=pl.BlockSpec(memory_space=pl.ANY),
        scratch_shapes=[
            pltpu.VMEM((HEADS, width), f32),
            pltpu.VMEM((HEADS, width), f32),
            pltpu.VMEM((1, width), jnp.int32),
            pltpu.VMEM((4, DK, span), bf16),
            pltpu.VMEM((HEADS, 8, width), f32),
            pltpu.VMEM((HEADS, 8, width), f32),
            pltpu.VMEM((span, span), f32),
            pltpu.VMEM((span, DK), bf16),
            pltpu.VMEM((span, DV), f32),
            pltpu.VMEM((span, 1), f32),
            pltpu.VMEM((PARTS, DK, 128), bf16),
            pltpu.VMEM((PARTS, DK, 128), bf16),
            pltpu.VMEM((24, DK), f32),
            pltpu.VMEM((24, DK), f32),
            pltpu.VMEM((HEADS, width, DV), bf16),
            dma((HEADS,)), dma((4,)), dma((HEADS - 1,)), dma((HEADS,)),
            dma((PARTS + 1,)), dma((PARTS + 1,)), dma((HEADS,)), dma((HEADS,)), dma((3,)),
        ],
        compiler_params=pltpu.CompilerParams(
            collective_id=0, has_side_effects=True, vmem_limit_bytes=60 * 1024 * 1024
        ),
    )(qkv, igate, fgate, doc_start.reshape(1, width), lengths)


def solution(mesh):
    placed = (
        P("seq", "groups"),
        P(None, ("groups", "seq")),
        P(None, ("groups", "seq")),
        P(("groups", "seq")),
        P(("groups", "seq")),
    )
    shards = mesh.shape["seq"]
    whole_heads = shards == HEADS * HEADS and shards * DK == 2 * HEADS * DK + HEADS * DV
    return jax.shard_map(
        worker_body if whole_heads else body, mesh=mesh, in_specs=placed, out_specs=P(("groups", "seq"), None), check_vma=False
    )
```

```python
import functools
import jax
import jax.numpy as jnp
from jax import lax
from jax.experimental import pallas as pl
from jax.experimental.pallas import tpu as pltpu
from jax.sharding import PartitionSpec as P

DK = 256
DV = 512
HEAD_COUNT_HALF = 4


empty_max = -1e30
highest = lax.Precision.HIGHEST


def running_sum(x):
    spots = lax.iota(jnp.int32, x.shape[-1])
    upto = spots[None, :] <= spots[:, None]
    return jnp.sum(jnp.where(upto, x[..., None, :], jnp.zeros((), x.dtype)), axis=-1)


def local_terms(queries, key_rows, value_rows, igate, fgate, doc_start, live_count):
    head_count, key_dim, width = queries.shape
    token_position = lax.iota(jnp.int32, width)
    living = token_position < live_count
    log_forget = jnp.where(living[None, :], jax.nn.log_sigmoid(fgate), 0.0)
    running = running_sum(log_forget)
    resets = running_sum(doc_start)
    allowed = (
        (resets[:, None] == resets[None, :])
        & (token_position[:, None] >= token_position[None, :])
        & living[None, :]
    )
    tail_doc = (resets == resets[width - 1]) & living
    key_scale = key_dim ** (-0.5)
    sums, denoms, squares, maxima = ([], [], [], [])
    states, normals, summary_sq, summary_max = ([], [], [], [])
    for head_index in range(head_count):
        exponent = (
            running[head_index][:, None] - running[head_index][None, :] + igate[head_index][None, :]
        )
        exponent = jnp.where(allowed, exponent, empty_max)
        row_max = jnp.max(exponent, axis=1)
        weights = jnp.where(allowed, jnp.exp(exponent - row_max[:, None]), 0.0)
        scores = (
            jnp.einsum(
                "dt,ds->ts",
                queries[head_index],
                key_rows[head_index],
                preferred_element_type=jnp.float32,
            )
            * key_scale
        )
        weighted = weights * scores
        sums.append(
            jnp.einsum(
                "ts,js->tj",
                weighted.astype(jnp.bfloat16),
                value_rows[head_index],
                preferred_element_type=jnp.float32,
            )
        )
        denoms.append(jnp.sum(weighted, axis=1))
        squares.append(jnp.sum(weights * weights, axis=1))
        maxima.append(row_max)
        closing = running[head_index][width - 1] - running[head_index] + igate[head_index]
        closing = jnp.where(tail_doc, closing, empty_max)
        largest = jnp.max(closing)
        carried = jnp.where(tail_doc, jnp.exp(closing - largest), 0.0)
        scaled_keys = (key_rows[head_index] * (carried * key_scale)[None, :]).astype(jnp.bfloat16)
        states.append(
            jnp.einsum(
                "ds,js->dj", scaled_keys, value_rows[head_index], preferred_element_type=jnp.float32
            )
        )
        normals.append(jnp.sum(scaled_keys.astype(jnp.float32), axis=1))
        summary_sq.append(jnp.sum(carried * carried))
        summary_max.append(largest)
    open_flag = jnp.where(resets[width - 1] == 0, 1.0, 0.0).astype(jnp.float32).reshape(1)
    local_parts = (
        jnp.stack(sums, axis=1),
        jnp.stack(denoms, axis=1),
        jnp.stack(squares, axis=1),
        jnp.stack(maxima, axis=1),
        running.T,
        resets == 0,
        living,
    )
    summary = (
        jnp.stack(states),
        jnp.stack(normals),
        jnp.stack(summary_sq),
        jnp.stack(summary_max),
        running[:, width - 1],
        open_flag,
    )
    return (local_parts, summary)


def finish(local_parts, incoming, queries):
    sums, denoms, squares, maxima, running, first_open, living = local_parts
    state_in, normal_in, square_in, max_in = (incoming[0], incoming[1], incoming[2], incoming[3])
    incoming_exp = jnp.where(first_open[:, None], running + max_in[None, :], empty_max)
    largest = jnp.maximum(maxima, incoming_exp)
    own_scale = jnp.exp(maxima - largest)
    carry_scale = jnp.where(first_open[:, None], jnp.exp(incoming_exp - largest), 0.0)
    cross_term = jnp.einsum(
        "hdt,hdj->thj", queries, state_in.astype(jnp.bfloat16), preferred_element_type=jnp.float32
    )
    cross_den = jnp.einsum(
        "hdt,hd->th", queries, normal_in.astype(jnp.bfloat16), preferred_element_type=jnp.float32
    )
    numerator = own_scale[..., None] * sums + carry_scale[..., None] * cross_term
    denominator = own_scale * denoms + carry_scale * cross_den
    square = own_scale * own_scale * squares + carry_scale * carry_scale * square_in[None, :]
    divisor = jnp.where(living[:, None], jnp.maximum(jnp.abs(denominator), jnp.sqrt(square)), 1.0)
    result = jnp.where(living[:, None, None], numerator / divisor[..., None], 0.0)
    return result.reshape(result.shape[0], -1).astype(jnp.bfloat16)


def spread_prefix(summary):
    states, normals, sq_sum, top_sum, tails, open_flag = summary
    shards = lax.axis_size("seq")
    own_index = lax.axis_index("seq")
    head_count, key_dim, value_dim = states.shape
    row_count = head_count * key_dim // shards
    spread = lax.all_to_all(
        states.reshape(1, head_count * key_dim, value_dim),
        "seq",
        split_axis=1,
        concat_axis=0,
        tiled=True,
    )
    normal_all, square_all, top_all, tail_all, open_all = (
        lax.all_gather(normals[None], "seq", axis=0, tiled=True),
        lax.all_gather(sq_sum[None], "seq", axis=0, tiled=True),
        lax.all_gather(top_sum[None], "seq", axis=0, tiled=True),
        lax.all_gather(tails[None], "seq", axis=0, tiled=True),
        lax.all_gather(open_flag, "seq", axis=0, tiled=True),
    )
    tails_after = running_sum(tail_all.T).T
    before = tails_after - tail_all
    closed_after = running_sum(1.0 - open_all)
    closed_before = closed_after - (1.0 - open_all)
    shard_order = lax.iota(jnp.int32, shards)
    linked = (shard_order[:, None] < shard_order[None, :]) & (
        closed_before[None, :] - closed_after[:, None] < 0.5
    )
    exponent = top_all[:, None, :] + before[None, :, :] - tails_after[:, None, :]
    exponent = jnp.where(linked[..., None], exponent, empty_max)
    entry_max = jnp.max(exponent, axis=0)
    weight = jnp.where(linked[..., None], jnp.exp(exponent - entry_max[None]), 0.0)
    own_pick = (shard_order == own_index).astype(jnp.float32)
    own_weight = jnp.einsum("ijh,j->ih", weight, own_pick, precision=highest)
    normal_in = jnp.einsum("ih,ihd->hd", own_weight, normal_all, precision=highest)
    square_in = jnp.einsum("ih,ih->h", own_weight * own_weight, square_all, precision=highest)
    max_in = jnp.einsum("jh,j->h", entry_max, own_pick, precision=highest)
    row_head = (own_index * row_count + lax.iota(jnp.int32, row_count)) // key_dim
    head_pick = (lax.iota(jnp.int32, head_count)[:, None] == row_head[None, :]).astype(jnp.float32)
    row_weight = jnp.einsum("ijh,hr->jir", weight, head_pick, precision=highest)
    state_rows = jnp.einsum("jir,irc->jrc", row_weight, spread, precision=highest)
    returned = lax.all_to_all(
        state_rows.astype(jnp.bfloat16), "seq", split_axis=0, concat_axis=1, tiled=True
    ).astype(state_rows.dtype)
    return (returned.reshape(head_count, key_dim, value_dim), normal_in, square_in, max_in)


def body(qkv, igate, fgate, doc_start, lengths):
    regrouped = lax.all_to_all(qkv, "seq", split_axis=1, concat_axis=0, tiled=True)
    width = igate.shape[1]
    queries = regrouped[: HEAD_COUNT_HALF * DK].reshape(HEAD_COUNT_HALF, DK, width)
    key_rows = regrouped[HEAD_COUNT_HALF * DK : 2 * HEAD_COUNT_HALF * DK].reshape(
        HEAD_COUNT_HALF, DK, width
    )
    value_rows = regrouped[2 * HEAD_COUNT_HALF * DK :].reshape(HEAD_COUNT_HALF, DV, width)
    local_parts, summary = local_terms(
        queries, key_rows, value_rows, igate, fgate, doc_start, lengths[0]
    )
    incoming = spread_prefix(summary)
    return finish(local_parts, incoming, queries)


MESH = pl.DeviceIdType.MESH
f32, bf16 = jnp.float32, jnp.bfloat16
HEADS = HEAD_COUNT_HALF
PARTS = DV // 128


def dot_nt(a, b):
    return lax.dot_general(a, b, (((1,), (1,)), ((), ())), preferred_element_type=f32)


def worker_kernel(
    qkv, ig_hbm, fg_hbm, doc_hbm, live_len, out,
    ig, fg, doc, inbox, meta, metain, top, sq_own, qt, num, den, st_in, st_out, sm_in, sm_out, obuf,
    insend, inrecv, msend, mrecv, csend, crecv, osend, orecv, lsem,
):
    planes = HEADS
    width = ig_hbm.shape[1]
    span = planes * width
    g = lax.axis_index("groups")
    d = lax.axis_index("seq")
    p = lax.div(d, HEADS)
    h = lax.rem(d, HEADS)
    big = lax.div(d, 2 * HEADS)
    hd = (1 - big) * h + big * (lax.div(d, 2) - HEADS)
    role = (1 - big) * p + big * (2 + lax.rem(d, 2))
    peers = [lax.rem(h + i, HEADS) for i in range(1, HEADS)]

    loads = [
        pltpu.make_async_copy(src, dst, lsem.at[i])
        for i, (src, dst) in enumerate(((ig_hbm, ig), (fg_hbm, fg), (doc_hbm, doc)))
    ]
    for c in loads:
        c.start()

    bar = pltpu.get_barrier_semaphore()

    def greet(dev):
        pl.semaphore_signal(bar, inc=1, device_id=(g, dev), device_id_type=MESH)

    for s in (h, HEADS + h, 2 * HEADS + 2 * h, 2 * HEADS + 2 * h + 1):
        pl.when(s != d)(functools.partial(greet, s))
    for b in peers:
        greet(HEADS * p + b)
    pl.when(p > 0)(functools.partial(greet, d - HEADS))

    for c in loads:
        c.wait()
    pos = lax.broadcasted_iota(jnp.int32, (1, width), 1)
    live = pos < live_len[0]
    x = fg[...]
    a = jnp.where(live, jnp.minimum(x, 0.0) - jnp.log1p(jnp.exp(-jnp.abs(x))), 0.0)
    livef = jnp.where(live, 1.0, 0.0).astype(f32)
    docf = doc[...].astype(f32)
    pad = jnp.zeros((4, width), f32)
    for i in range(HEADS):
        meta[i] = jnp.concatenate([ig[i : i + 1, :], a[i : i + 1, :], docf, livef, pad], axis=0)

    count = 2 * HEADS - 1 + jnp.where(p < planes - 1, 1, 0) - jnp.where(hd == h, 1, 0)
    pl.semaphore_wait(bar, count)

    def remote(src, dst, ss, rs, dev):
        return pltpu.make_async_remote_copy(
            src_ref=src, dst_ref=dst, send_sem=ss, recv_sem=rs, device_id=(g, dev), device_id_type=MESH
        )

    mcopies = [
        remote(meta.at[b], metain.at[h], msend.at[i], mrecv.at[h], HEADS * p + b)
        for i, b in enumerate(peers)
    ]
    for c in mcopies:
        c.start()
    metain[h] = meta[h]

    def feature(j):
        return remote(
            qkv.at[:, pl.ds(j * span, span)], inbox.at[role], insend.at[j], inrecv.at[role], HEADS * j + hd
        )

    for j in range(planes):
        away = HEADS * j + hd != d

        @pl.when(away)
        def _():
            feature(j).start()

        @pl.when(jnp.logical_not(away))
        def _():
            pltpu.make_async_copy(
                qkv.at[:, pl.ds(j * span, span)], inbox.at[role], inrecv.at[role]
            ).start()

    def landed(slot):
        pltpu.make_async_copy(inbox.at[slot], inbox.at[slot], inrecv.at[slot]).wait()

    for i, b in enumerate(peers):
        pltpu.make_async_copy(metain.at[b], metain.at[b], mrecv.at[b]).wait()

    ti = lax.broadcasted_iota(jnp.int32, (width, width), 0)
    si = lax.broadcasted_iota(jnp.int32, (width, width), 1)
    eye = ti == si

    def upright(row):
        return jnp.sum(jnp.where(eye, row, 0.0), axis=1, keepdims=True)

    b_cols, r_cols, live_cols, b_rows, r_rows = [], [], [], [], []
    b_last = r_last = jnp.zeros((1, 1), f32)
    for i in range(planes):
        gates = metain[i]
        for at, last, cols, lines in ((1, b_last, b_cols, b_rows), (2, r_last, r_cols, r_rows)):
            col = last + jnp.sum(jnp.where(ti >= si, gates[at : at + 1], 0.0), axis=1, keepdims=True)
            cols.append(col)
            lines.append(jnp.sum(jnp.where(eye, col, 0.0), axis=0, keepdims=True))
        b_last, r_last = b_rows[-1][:, width - 1 :], r_rows[-1][:, width - 1 :]
        live_cols.append(upright(gates[3:4]))
    b_row, r_row = jnp.concatenate(b_rows, axis=1), jnp.concatenate(r_rows, axis=1)
    ig_row = jnp.concatenate([metain[i, 0:1, :] for i in range(planes)], axis=1)
    live_row = jnp.concatenate([metain[i, 3:4, :] for i in range(planes)], axis=1)
    b_end = b_row[:, span - 1 : span]
    r_end = r_row[:, span - 1 : span]
    tail = (r_row == r_end) & (live_row > 0.5)
    cl = jnp.where(tail, b_end - b_row + ig_row, empty_max)
    mu = jnp.max(cl, axis=1, keepdims=True)
    u = jnp.where(tail, jnp.exp(cl - mu), 0.0)
    sq_sum = jnp.sum(u * u, axis=1, keepdims=True)
    key_scale = DK ** (-0.5)

    def own():
        landed(0)
        qt[...] = inbox[0].astype(f32).T.astype(bf16)
        for b in range(planes):
            r = pl.ds(b * width, width)
            wide = (b + 1) * width
            row_at = b * width + lax.broadcasted_iota(jnp.int32, (width, wide), 0)
            col_at = lax.broadcasted_iota(jnp.int32, (width, wide), 1)
            allowed = (row_at >= col_at) & (r_cols[b] == r_row[:, :wide]) & (live_row[:, :wide] > 0.5)
            ex = jnp.where(allowed, b_cols[b] - b_row[:, :wide] + ig_row[:, :wide], empty_max)
            highest_ex = jnp.max(ex, axis=1, keepdims=True)
            weights = jnp.where(allowed, jnp.exp(ex - highest_ex), 0.0)
            top[r, :] = highest_ex
            sq_own[r, :] = jnp.sum(weights * weights, axis=1, keepdims=True)
            score = jnp.dot(qt[r, :], inbox[1, :, 0:wide], preferred_element_type=f32) * key_scale
            w = weights * score
            den[r, :] = jnp.sum(w, axis=1, keepdims=True)
            wb = w.astype(bf16)
            for f in range(2):
                num[r, pl.ds(f * DK, DK)] = dot_nt(wb, inbox[2 + f, :, 0:wide])

    @pl.when(p == 0)
    def _():
        st_in[...] = jnp.zeros(st_in.shape, bf16)
        sm_in[...] = jnp.concatenate(
            [jnp.zeros((16, DK), f32), jnp.full((8, DK), empty_max, f32)], axis=0
        )

    landed(1)
    keyw = (inbox[1].astype(f32) * (u * key_scale)).astype(bf16)
    n8 = dot_nt(jnp.ones((8, span), bf16), keyw)
    landed(2)
    landed(3)
    pl.when(p >= 2)(own)

    sm_copy = remote(sm_out, sm_in, csend.at[PARTS], crecv.at[PARTS], d + HEADS)
    st_copies = [
        remote(st_out.at[c], st_in.at[c], csend.at[c], crecv.at[c], d + HEADS) for c in range(PARTS)
    ]

    @pl.when(p > 0)
    def _():
        pltpu.make_async_copy(sm_in, sm_in, crecv.at[PARTS]).wait()

    m_in = sm_in[16:17, 0:1]
    carried = b_end + m_in
    opened = r_end < 0.5
    largest = jnp.maximum(mu, jnp.where(opened, carried, empty_max))
    late = jnp.exp(mu - largest)
    early = jnp.where(opened, jnp.exp(carried - largest), 0.0)

    @pl.when(p < planes - 1)
    def _():
        sm_out[0:8, :] = late * n8 + early * sm_in[0:8, :]
        sm_out[8:16, :] = late * late * sq_sum + early * early * sm_in[8:16, :]
        sm_out[16:24, :] = jnp.broadcast_to(largest, (8, DK))
        sm_copy.start()

    for c in range(PARTS):

        @pl.when(p > 0)
        def _():
            pltpu.make_async_copy(st_in.at[c], st_in.at[c], crecv.at[c]).wait()

        @pl.when(p < planes - 1)
        def _():
            vals = inbox[2 + c // 2, pl.ds((c % 2) * 128, 128), :]
            st_out[c] = (late * dot_nt(keyw, vals) + early * st_in[c].astype(f32)).astype(bf16)
            st_copies[c].start()

    pl.when(p < 2)(own)

    nb = sm_in[0:8, :].astype(bf16)
    sq_in = sm_in[8:9, 0:1]

    def result(b):
        return remote(
            obuf.at[b], out.at[:, pl.ds(pl.multiple_of(h * DV, DV), DV)], osend.at[b], orecv.at[h], HEADS * p + b
        )

    def own_result(b):
        return pltpu.make_async_copy(
            obuf.at[b], out.at[:, pl.ds(pl.multiple_of(h * DV, DV), DV)], orecv.at[h]
        )

    for b in range(planes):
        r = pl.ds(b * width, width)
        first = r_cols[b] < 0.5
        f = jnp.where(first, b_cols[b] + m_in, empty_max)
        mx = top[r, :]
        m = jnp.maximum(mx, f)
        xs = jnp.exp(mx - m)
        ys = jnp.where(first, jnp.exp(f - m), 0.0)
        qb = qt[r, :]
        dn = xs * den[r, :] + ys * dot_nt(qb, nb)[:, 0:1]
        sq = xs * xs * sq_own[r, :] + ys * ys * sq_in
        lv = live_cols[b] > 0.5
        inv = 1.0 / jnp.where(lv, jnp.maximum(jnp.abs(dn), jnp.sqrt(sq)), 1.0)
        for c in range(PARTS):
            cs = pl.ds(c * 128, 128)
            cross = jnp.dot(qb, st_in[c], preferred_element_type=f32)
            obuf[b, :, cs] = jnp.where(lv, (xs * num[r, cs] + ys * cross) * inv, 0.0).astype(bf16)

        @pl.when(h != b)
        def _():
            result(b).start()

        @pl.when(h == b)
        def _():
            own_result(b).start()

    for i in range(HEADS):
        here = out.at[:, pl.ds(i * DV, DV)]
        pltpu.make_async_copy(here, here, orecv.at[i]).wait()
    for c in mcopies:
        c.wait_send()
    for j in range(planes):

        @pl.when(HEADS * j + hd != d)
        def _():
            feature(j).wait_send()

        @pl.when(h != j)
        def _():
            result(j).wait_send()

    @pl.when(p < planes - 1)
    def _():
        sm_copy.wait_send()
        for c in st_copies:
            c.wait_send()


def worker_body(qkv, igate, fgate, doc_start, lengths):
    width = igate.shape[1]
    span = HEADS * width
    anywhere = pl.BlockSpec(memory_space=pl.ANY)
    dma = pltpu.SemaphoreType.DMA
    return pl.pallas_call(
        worker_kernel,
        out_shape=jax.ShapeDtypeStruct((width, HEADS * DV), bf16),
        in_specs=[anywhere] * 4 + [pl.BlockSpec(memory_space=pltpu.SMEM)],
        out_specs=pl.BlockSpec(memory_space=pl.ANY),
        scratch_shapes=[
            pltpu.VMEM((HEADS, width), f32),
            pltpu.VMEM((HEADS, width), f32),
            pltpu.VMEM((1, width), jnp.int32),
            pltpu.VMEM((4, DK, span), bf16),
            pltpu.VMEM((HEADS, 8, width), f32),
            pltpu.VMEM((HEADS, 8, width), f32),
            pltpu.VMEM((span, 1), f32),
            pltpu.VMEM((span, 1), f32),
            pltpu.VMEM((span, DK), bf16),
            pltpu.VMEM((span, DV), f32),
            pltpu.VMEM((span, 1), f32),
            pltpu.VMEM((PARTS, DK, 128), bf16),
            pltpu.VMEM((PARTS, DK, 128), bf16),
            pltpu.VMEM((24, DK), f32),
            pltpu.VMEM((24, DK), f32),
            pltpu.VMEM((HEADS, width, DV), bf16),
            dma((HEADS,)), dma((4,)), dma((HEADS - 1,)), dma((HEADS,)),
            dma((PARTS + 1,)), dma((PARTS + 1,)), dma((HEADS,)), dma((HEADS,)), dma((3,)),
        ],
        compiler_params=pltpu.CompilerParams(
            collective_id=0, has_side_effects=True, vmem_limit_bytes=60 * 1024 * 1024
        ),
    )(qkv, igate, fgate, doc_start.reshape(1, width), lengths)


def solution(mesh):
    placed = (
        P("seq", "groups"),
        P(None, ("groups", "seq")),
        P(None, ("groups", "seq")),
        P(("groups", "seq")),
        P(("groups", "seq")),
    )
    shards = mesh.shape["seq"]
    whole_heads = shards == HEADS * HEADS and shards * DK == 2 * HEADS * DK + HEADS * DV
    return jax.shard_map(
        worker_body if whole_heads else body, mesh=mesh, in_specs=placed, out_specs=P(("groups", "seq"), None), check_vma=False
    )
```

```python
import functools
import jax
import jax.numpy as jnp
from jax import lax
from jax.experimental import pallas as pl
from jax.experimental.pallas import tpu as pltpu
from jax.sharding import PartitionSpec as P

DK = 256
DV = 512
HEAD_COUNT_HALF = 4


empty_max = -1e30
highest = lax.Precision.HIGHEST


def running_sum(x):
    spots = lax.iota(jnp.int32, x.shape[-1])
    upto = spots[None, :] <= spots[:, None]
    return jnp.sum(jnp.where(upto, x[..., None, :], jnp.zeros((), x.dtype)), axis=-1)


def local_terms(queries, key_rows, value_rows, igate, fgate, doc_start, live_count):
    head_count, key_dim, width = queries.shape
    token_position = lax.iota(jnp.int32, width)
    living = token_position < live_count
    log_forget = jnp.where(living[None, :], jax.nn.log_sigmoid(fgate), 0.0)
    running = running_sum(log_forget)
    resets = running_sum(doc_start)
    allowed = (
        (resets[:, None] == resets[None, :])
        & (token_position[:, None] >= token_position[None, :])
        & living[None, :]
    )
    tail_doc = (resets == resets[width - 1]) & living
    key_scale = key_dim ** (-0.5)
    sums, denoms, squares, maxima = ([], [], [], [])
    states, normals, summary_sq, summary_max = ([], [], [], [])
    for head_index in range(head_count):
        exponent = (
            running[head_index][:, None] - running[head_index][None, :] + igate[head_index][None, :]
        )
        exponent = jnp.where(allowed, exponent, empty_max)
        row_max = jnp.max(exponent, axis=1)
        weights = jnp.where(allowed, jnp.exp(exponent - row_max[:, None]), 0.0)
        scores = (
            jnp.einsum(
                "dt,ds->ts",
                queries[head_index],
                key_rows[head_index],
                preferred_element_type=jnp.float32,
            )
            * key_scale
        )
        weighted = weights * scores
        sums.append(
            jnp.einsum(
                "ts,js->tj",
                weighted.astype(jnp.bfloat16),
                value_rows[head_index],
                preferred_element_type=jnp.float32,
            )
        )
        denoms.append(jnp.sum(weighted, axis=1))
        squares.append(jnp.sum(weights * weights, axis=1))
        maxima.append(row_max)
        closing = running[head_index][width - 1] - running[head_index] + igate[head_index]
        closing = jnp.where(tail_doc, closing, empty_max)
        largest = jnp.max(closing)
        carried = jnp.where(tail_doc, jnp.exp(closing - largest), 0.0)
        scaled_keys = (key_rows[head_index] * (carried * key_scale)[None, :]).astype(jnp.bfloat16)
        states.append(
            jnp.einsum(
                "ds,js->dj", scaled_keys, value_rows[head_index], preferred_element_type=jnp.float32
            )
        )
        normals.append(jnp.sum(scaled_keys.astype(jnp.float32), axis=1))
        summary_sq.append(jnp.sum(carried * carried))
        summary_max.append(largest)
    open_flag = jnp.where(resets[width - 1] == 0, 1.0, 0.0).astype(jnp.float32).reshape(1)
    local_parts = (
        jnp.stack(sums, axis=1),
        jnp.stack(denoms, axis=1),
        jnp.stack(squares, axis=1),
        jnp.stack(maxima, axis=1),
        running.T,
        resets == 0,
        living,
    )
    summary = (
        jnp.stack(states),
        jnp.stack(normals),
        jnp.stack(summary_sq),
        jnp.stack(summary_max),
        running[:, width - 1],
        open_flag,
    )
    return (local_parts, summary)


def finish(local_parts, incoming, queries):
    sums, denoms, squares, maxima, running, first_open, living = local_parts
    state_in, normal_in, square_in, max_in = (incoming[0], incoming[1], incoming[2], incoming[3])
    incoming_exp = jnp.where(first_open[:, None], running + max_in[None, :], empty_max)
    largest = jnp.maximum(maxima, incoming_exp)
    own_scale = jnp.exp(maxima - largest)
    carry_scale = jnp.where(first_open[:, None], jnp.exp(incoming_exp - largest), 0.0)
    cross_term = jnp.einsum(
        "hdt,hdj->thj", queries, state_in.astype(jnp.bfloat16), preferred_element_type=jnp.float32
    )
    cross_den = jnp.einsum(
        "hdt,hd->th", queries, normal_in.astype(jnp.bfloat16), preferred_element_type=jnp.float32
    )
    numerator = own_scale[..., None] * sums + carry_scale[..., None] * cross_term
    denominator = own_scale * denoms + carry_scale * cross_den
    square = own_scale * own_scale * squares + carry_scale * carry_scale * square_in[None, :]
    divisor = jnp.where(living[:, None], jnp.maximum(jnp.abs(denominator), jnp.sqrt(square)), 1.0)
    result = jnp.where(living[:, None, None], numerator / divisor[..., None], 0.0)
    return result.reshape(result.shape[0], -1).astype(jnp.bfloat16)


def spread_prefix(summary):
    states, normals, sq_sum, top_sum, tails, open_flag = summary
    shards = lax.axis_size("seq")
    own_index = lax.axis_index("seq")
    head_count, key_dim, value_dim = states.shape
    row_count = head_count * key_dim // shards
    spread = lax.all_to_all(
        states.reshape(1, head_count * key_dim, value_dim),
        "seq",
        split_axis=1,
        concat_axis=0,
        tiled=True,
    )
    normal_all, square_all, top_all, tail_all, open_all = (
        lax.all_gather(normals[None], "seq", axis=0, tiled=True),
        lax.all_gather(sq_sum[None], "seq", axis=0, tiled=True),
        lax.all_gather(top_sum[None], "seq", axis=0, tiled=True),
        lax.all_gather(tails[None], "seq", axis=0, tiled=True),
        lax.all_gather(open_flag, "seq", axis=0, tiled=True),
    )
    tails_after = running_sum(tail_all.T).T
    before = tails_after - tail_all
    closed_after = running_sum(1.0 - open_all)
    closed_before = closed_after - (1.0 - open_all)
    shard_order = lax.iota(jnp.int32, shards)
    linked = (shard_order[:, None] < shard_order[None, :]) & (
        closed_before[None, :] - closed_after[:, None] < 0.5
    )
    exponent = top_all[:, None, :] + before[None, :, :] - tails_after[:, None, :]
    exponent = jnp.where(linked[..., None], exponent, empty_max)
    entry_max = jnp.max(exponent, axis=0)
    weight = jnp.where(linked[..., None], jnp.exp(exponent - entry_max[None]), 0.0)
    own_pick = (shard_order == own_index).astype(jnp.float32)
    own_weight = jnp.einsum("ijh,j->ih", weight, own_pick, precision=highest)
    normal_in = jnp.einsum("ih,ihd->hd", own_weight, normal_all, precision=highest)
    square_in = jnp.einsum("ih,ih->h", own_weight * own_weight, square_all, precision=highest)
    max_in = jnp.einsum("jh,j->h", entry_max, own_pick, precision=highest)
    row_head = (own_index * row_count + lax.iota(jnp.int32, row_count)) // key_dim
    head_pick = (lax.iota(jnp.int32, head_count)[:, None] == row_head[None, :]).astype(jnp.float32)
    row_weight = jnp.einsum("ijh,hr->jir", weight, head_pick, precision=highest)
    state_rows = jnp.einsum("jir,irc->jrc", row_weight, spread, precision=highest)
    returned = lax.all_to_all(
        state_rows.astype(jnp.bfloat16), "seq", split_axis=0, concat_axis=1, tiled=True
    ).astype(state_rows.dtype)
    return (returned.reshape(head_count, key_dim, value_dim), normal_in, square_in, max_in)


def body(qkv, igate, fgate, doc_start, lengths):
    regrouped = lax.all_to_all(qkv, "seq", split_axis=1, concat_axis=0, tiled=True)
    width = igate.shape[1]
    queries = regrouped[: HEAD_COUNT_HALF * DK].reshape(HEAD_COUNT_HALF, DK, width)
    key_rows = regrouped[HEAD_COUNT_HALF * DK : 2 * HEAD_COUNT_HALF * DK].reshape(
        HEAD_COUNT_HALF, DK, width
    )
    value_rows = regrouped[2 * HEAD_COUNT_HALF * DK :].reshape(HEAD_COUNT_HALF, DV, width)
    local_parts, summary = local_terms(
        queries, key_rows, value_rows, igate, fgate, doc_start, lengths[0]
    )
    incoming = spread_prefix(summary)
    return finish(local_parts, incoming, queries)


MESH = pl.DeviceIdType.MESH
f32, bf16 = jnp.float32, jnp.bfloat16
HEADS = HEAD_COUNT_HALF
PARTS = DV // 128


def dot_nt(a, b):
    return lax.dot_general(a, b, (((1,), (1,)), ((), ())), preferred_element_type=f32)


def worker_kernel(
    qkv, ig_hbm, fg_hbm, doc_hbm, live_len, out,
    ig, fg, doc, inbox, meta, metain, top, sq_own, qt, num, den, st_in, st_out, sm_in, sm_out, obuf,
    insend, inrecv, msend, mrecv, csend, crecv, osend, orecv, lsem,
):
    planes = HEADS
    width = ig_hbm.shape[1]
    span = planes * width
    g = lax.axis_index("groups")
    d = lax.axis_index("seq")
    p = lax.div(d, HEADS)
    h = lax.rem(d, HEADS)
    big = lax.div(d, 2 * HEADS)
    hd = (1 - big) * h + big * (lax.div(d, 2) - HEADS)
    role = (1 - big) * p + big * (2 + lax.rem(d, 2))
    peers = [lax.rem(h + i, HEADS) for i in range(1, HEADS)]

    loads = [
        pltpu.make_async_copy(src, dst, lsem.at[i])
        for i, (src, dst) in enumerate(((ig_hbm, ig), (fg_hbm, fg), (doc_hbm, doc)))
    ]
    for c in loads:
        c.start()

    bar = pltpu.get_barrier_semaphore()

    def greet(dev):
        pl.semaphore_signal(bar, inc=1, device_id=(g, dev), device_id_type=MESH)

    for s in (h, HEADS + h, 2 * HEADS + 2 * h, 2 * HEADS + 2 * h + 1):
        pl.when(s != d)(functools.partial(greet, s))
    for b in peers:
        greet(HEADS * p + b)
    pl.when(p > 0)(functools.partial(greet, d - HEADS))

    for c in loads:
        c.wait()
    pos = lax.broadcasted_iota(jnp.int32, (1, width), 1)
    live = pos < live_len[0]
    x = fg[...]
    a = jnp.where(live, jnp.minimum(x, 0.0) - jnp.log1p(jnp.exp(-jnp.abs(x))), 0.0)
    livef = jnp.where(live, 1.0, 0.0).astype(f32)
    docf = doc[...].astype(f32)
    pad = jnp.zeros((4, width), f32)
    for i in range(HEADS):
        meta[i] = jnp.concatenate([ig[i : i + 1, :], a[i : i + 1, :], docf, livef, pad], axis=0)

    count = 2 * HEADS - 1 + jnp.where(p < planes - 1, 1, 0) - jnp.where(hd == h, 1, 0)
    pl.semaphore_wait(bar, count)

    def remote(src, dst, ss, rs, dev):
        return pltpu.make_async_remote_copy(
            src_ref=src, dst_ref=dst, send_sem=ss, recv_sem=rs, device_id=(g, dev), device_id_type=MESH
        )

    mcopies = [
        remote(meta.at[b], metain.at[h], msend.at[i], mrecv.at[h], HEADS * p + b)
        for i, b in enumerate(peers)
    ]
    for c in mcopies:
        c.start()
    metain[h] = meta[h]

    def feature(j):
        return remote(
            qkv.at[:, pl.ds(j * span, span)], inbox.at[role], insend.at[j], inrecv.at[role], HEADS * j + hd
        )

    def send(j):
        away = HEADS * j + hd != d

        @pl.when(away)
        def _():
            feature(j).start()

        @pl.when(jnp.logical_not(away))
        def _():
            pltpu.make_async_copy(
                qkv.at[:, pl.ds(j * span, span)], inbox.at[role], inrecv.at[role]
            ).start()

    def send_rest():
        for j in range(1, planes):
            send(j)

    send(0)
    pl.when(big == 0)(send_rest)

    def landed(slot):
        pltpu.make_async_copy(inbox.at[slot], inbox.at[slot], inrecv.at[slot]).wait()

    for i, b in enumerate(peers):
        pltpu.make_async_copy(metain.at[b], metain.at[b], mrecv.at[b]).wait()

    ti = lax.broadcasted_iota(jnp.int32, (width, width), 0)
    si = lax.broadcasted_iota(jnp.int32, (width, width), 1)
    eye = ti == si

    def upright(row):
        return jnp.sum(jnp.where(eye, row, 0.0), axis=1, keepdims=True)

    b_cols, r_cols, live_cols, b_rows, r_rows = [], [], [], [], []
    b_last = r_last = jnp.zeros((1, 1), f32)
    for i in range(planes):
        gates = metain[i]
        for at, last, cols, lines in ((1, b_last, b_cols, b_rows), (2, r_last, r_cols, r_rows)):
            col = last + jnp.sum(jnp.where(ti >= si, gates[at : at + 1], 0.0), axis=1, keepdims=True)
            cols.append(col)
            lines.append(jnp.sum(jnp.where(eye, col, 0.0), axis=0, keepdims=True))
        b_last, r_last = b_rows[-1][:, width - 1 :], r_rows[-1][:, width - 1 :]
        live_cols.append(upright(gates[3:4]))
    b_row, r_row = jnp.concatenate(b_rows, axis=1), jnp.concatenate(r_rows, axis=1)
    ig_row = jnp.concatenate([metain[i, 0:1, :] for i in range(planes)], axis=1)
    live_row = jnp.concatenate([metain[i, 3:4, :] for i in range(planes)], axis=1)
    b_end = b_row[:, span - 1 : span]
    r_end = r_row[:, span - 1 : span]
    tail = (r_row == r_end) & (live_row > 0.5)
    cl = jnp.where(tail, b_end - b_row + ig_row, empty_max)
    mu = jnp.max(cl, axis=1, keepdims=True)
    u = jnp.where(tail, jnp.exp(cl - mu), 0.0)
    sq_sum = jnp.sum(u * u, axis=1, keepdims=True)
    key_scale = DK ** (-0.5)

    @pl.when(big > 0)
    def _():
        feature(0).wait_send()
        send_rest()

    def own():
        landed(0)
        qt[...] = inbox[0].astype(f32).T.astype(bf16)
        for b in range(planes):
            r = pl.ds(b * width, width)
            wide = (b + 1) * width
            row_at = b * width + lax.broadcasted_iota(jnp.int32, (width, wide), 0)
            col_at = lax.broadcasted_iota(jnp.int32, (width, wide), 1)
            allowed = (row_at >= col_at) & (r_cols[b] == r_row[:, :wide]) & (live_row[:, :wide] > 0.5)
            ex = jnp.where(allowed, b_cols[b] - b_row[:, :wide] + ig_row[:, :wide], empty_max)
            highest_ex = jnp.max(ex, axis=1, keepdims=True)
            weights = jnp.where(allowed, jnp.exp(ex - highest_ex), 0.0)
            top[r, :] = highest_ex
            sq_own[r, :] = jnp.sum(weights * weights, axis=1, keepdims=True)
            score = jnp.dot(qt[r, :], inbox[1, :, 0:wide], preferred_element_type=f32) * key_scale
            w = weights * score
            den[r, :] = jnp.sum(w, axis=1, keepdims=True)
            wb = w.astype(bf16)
            for f in range(2):
                num[r, pl.ds(f * DK, DK)] = dot_nt(wb, inbox[2 + f, :, 0:wide])

    @pl.when(p == 0)
    def _():
        st_in[...] = jnp.zeros(st_in.shape, bf16)
        sm_in[...] = jnp.concatenate(
            [jnp.zeros((16, DK), f32), jnp.full((8, DK), empty_max, f32)], axis=0
        )

    landed(1)
    keyw = (inbox[1].astype(f32) * (u * key_scale)).astype(bf16)
    n8 = dot_nt(jnp.ones((8, span), bf16), keyw)
    landed(2)
    landed(3)
    pl.when(p >= 2)(own)

    sm_copy = remote(sm_out, sm_in, csend.at[PARTS], crecv.at[PARTS], d + HEADS)
    st_copies = [
        remote(st_out.at[c], st_in.at[c], csend.at[c], crecv.at[c], d + HEADS) for c in range(PARTS)
    ]

    @pl.when(p > 0)
    def _():
        pltpu.make_async_copy(sm_in, sm_in, crecv.at[PARTS]).wait()

    m_in = sm_in[16:17, 0:1]
    carried = b_end + m_in
    opened = r_end < 0.5
    largest = jnp.maximum(mu, jnp.where(opened, carried, empty_max))
    late = jnp.exp(mu - largest)
    early = jnp.where(opened, jnp.exp(carried - largest), 0.0)

    @pl.when(p < planes - 1)
    def _():
        sm_out[0:8, :] = late * n8 + early * sm_in[0:8, :]
        sm_out[8:16, :] = late * late * sq_sum + early * early * sm_in[8:16, :]
        sm_out[16:24, :] = jnp.broadcast_to(largest, (8, DK))
        sm_copy.start()

    for c in range(PARTS):

        @pl.when(p > 0)
        def _():
            pltpu.make_async_copy(st_in.at[c], st_in.at[c], crecv.at[c]).wait()

        @pl.when(p < planes - 1)
        def _():
            vals = inbox[2 + c // 2, pl.ds((c % 2) * 128, 128), :]
            st_out[c] = (late * dot_nt(keyw, vals) + early * st_in[c].astype(f32)).astype(bf16)
            st_copies[c].start()

    pl.when(p < 2)(own)

    nb = sm_in[0:8, :].astype(bf16)
    sq_in = sm_in[8:9, 0:1]

    def result(b):
        return remote(
            obuf.at[b], out.at[:, pl.ds(pl.multiple_of(h * DV, DV), DV)], osend.at[b], orecv.at[h], HEADS * p + b
        )

    def own_result(b):
        return pltpu.make_async_copy(
            obuf.at[b], out.at[:, pl.ds(pl.multiple_of(h * DV, DV), DV)], orecv.at[h]
        )

    for b in range(planes):
        r = pl.ds(b * width, width)
        first = r_cols[b] < 0.5
        f = jnp.where(first, b_cols[b] + m_in, empty_max)
        mx = top[r, :]
        m = jnp.maximum(mx, f)
        xs = jnp.exp(mx - m)
        ys = jnp.where(first, jnp.exp(f - m), 0.0)
        qb = qt[r, :]
        dn = xs * den[r, :] + ys * dot_nt(qb, nb)[:, 0:1]
        sq = xs * xs * sq_own[r, :] + ys * ys * sq_in
        lv = live_cols[b] > 0.5
        inv = 1.0 / jnp.where(lv, jnp.maximum(jnp.abs(dn), jnp.sqrt(sq)), 1.0)
        for c in range(PARTS):
            cs = pl.ds(c * 128, 128)
            cross = jnp.dot(qb, st_in[c], preferred_element_type=f32)
            obuf[b, :, cs] = jnp.where(lv, (xs * num[r, cs] + ys * cross) * inv, 0.0).astype(bf16)

        @pl.when(h != b)
        def _():
            result(b).start()

        @pl.when(h == b)
        def _():
            own_result(b).start()

    for i in range(HEADS):
        here = out.at[:, pl.ds(i * DV, DV)]
        pltpu.make_async_copy(here, here, orecv.at[i]).wait()
    for c in mcopies:
        c.wait_send()
    for j in range(planes):

        @pl.when((HEADS * j + hd != d) & (big * (planes - j) < planes))
        def _():
            feature(j).wait_send()

        @pl.when(h != j)
        def _():
            result(j).wait_send()

    @pl.when(p < planes - 1)
    def _():
        sm_copy.wait_send()
        for c in st_copies:
            c.wait_send()


def worker_body(qkv, igate, fgate, doc_start, lengths):
    width = igate.shape[1]
    span = HEADS * width
    anywhere = pl.BlockSpec(memory_space=pl.ANY)
    dma = pltpu.SemaphoreType.DMA
    return pl.pallas_call(
        worker_kernel,
        out_shape=jax.ShapeDtypeStruct((width, HEADS * DV), bf16),
        in_specs=[anywhere] * 4 + [pl.BlockSpec(memory_space=pltpu.SMEM)],
        out_specs=pl.BlockSpec(memory_space=pl.ANY),
        scratch_shapes=[
            pltpu.VMEM((HEADS, width), f32),
            pltpu.VMEM((HEADS, width), f32),
            pltpu.VMEM((1, width), jnp.int32),
            pltpu.VMEM((4, DK, span), bf16),
            pltpu.VMEM((HEADS, 8, width), f32),
            pltpu.VMEM((HEADS, 8, width), f32),
            pltpu.VMEM((span, 1), f32),
            pltpu.VMEM((span, 1), f32),
            pltpu.VMEM((span, DK), bf16),
            pltpu.VMEM((span, DV), f32),
            pltpu.VMEM((span, 1), f32),
            pltpu.VMEM((PARTS, DK, 128), bf16),
            pltpu.VMEM((PARTS, DK, 128), bf16),
            pltpu.VMEM((24, DK), f32),
            pltpu.VMEM((24, DK), f32),
            pltpu.VMEM((HEADS, width, DV), bf16),
            dma((HEADS,)), dma((4,)), dma((HEADS - 1,)), dma((HEADS,)),
            dma((PARTS + 1,)), dma((PARTS + 1,)), dma((HEADS,)), dma((HEADS,)), dma((3,)),
        ],
        compiler_params=pltpu.CompilerParams(
            collective_id=0, has_side_effects=True, vmem_limit_bytes=60 * 1024 * 1024
        ),
    )(qkv, igate, fgate, doc_start.reshape(1, width), lengths)


def solution(mesh):
    placed = (
        P("seq", "groups"),
        P(None, ("groups", "seq")),
        P(None, ("groups", "seq")),
        P(("groups", "seq")),
        P(("groups", "seq")),
    )
    shards = mesh.shape["seq"]
    whole_heads = shards == HEADS * HEADS and shards * DK == 2 * HEADS * DK + HEADS * DV
    return jax.shard_map(
        worker_body if whole_heads else body, mesh=mesh, in_specs=placed, out_specs=P(("groups", "seq"), None), check_vma=False
    )
```

```python
import functools
import jax
import jax.numpy as jnp
from jax import lax
from jax.experimental import pallas as pl
from jax.experimental.pallas import tpu as pltpu
from jax.sharding import PartitionSpec as P

DK = 256
DV = 512
HEAD_COUNT_HALF = 4


empty_max = -1e30
highest = lax.Precision.HIGHEST


def running_sum(x):
    spots = lax.iota(jnp.int32, x.shape[-1])
    upto = spots[None, :] <= spots[:, None]
    return jnp.sum(jnp.where(upto, x[..., None, :], jnp.zeros((), x.dtype)), axis=-1)


def local_terms(queries, key_rows, value_rows, igate, fgate, doc_start, live_count):
    head_count, key_dim, width = queries.shape
    token_position = lax.iota(jnp.int32, width)
    living = token_position < live_count
    log_forget = jnp.where(living[None, :], jax.nn.log_sigmoid(fgate), 0.0)
    running = running_sum(log_forget)
    resets = running_sum(doc_start)
    allowed = (
        (resets[:, None] == resets[None, :])
        & (token_position[:, None] >= token_position[None, :])
        & living[None, :]
    )
    tail_doc = (resets == resets[width - 1]) & living
    key_scale = key_dim ** (-0.5)
    sums, denoms, squares, maxima = ([], [], [], [])
    states, normals, summary_sq, summary_max = ([], [], [], [])
    for head_index in range(head_count):
        exponent = (
            running[head_index][:, None] - running[head_index][None, :] + igate[head_index][None, :]
        )
        exponent = jnp.where(allowed, exponent, empty_max)
        row_max = jnp.max(exponent, axis=1)
        weights = jnp.where(allowed, jnp.exp(exponent - row_max[:, None]), 0.0)
        scores = (
            jnp.einsum(
                "dt,ds->ts",
                queries[head_index],
                key_rows[head_index],
                preferred_element_type=jnp.float32,
            )
            * key_scale
        )
        weighted = weights * scores
        sums.append(
            jnp.einsum(
                "ts,js->tj",
                weighted.astype(jnp.bfloat16),
                value_rows[head_index],
                preferred_element_type=jnp.float32,
            )
        )
        denoms.append(jnp.sum(weighted, axis=1))
        squares.append(jnp.sum(weights * weights, axis=1))
        maxima.append(row_max)
        closing = running[head_index][width - 1] - running[head_index] + igate[head_index]
        closing = jnp.where(tail_doc, closing, empty_max)
        largest = jnp.max(closing)
        carried = jnp.where(tail_doc, jnp.exp(closing - largest), 0.0)
        scaled_keys = (key_rows[head_index] * (carried * key_scale)[None, :]).astype(jnp.bfloat16)
        states.append(
            jnp.einsum(
                "ds,js->dj", scaled_keys, value_rows[head_index], preferred_element_type=jnp.float32
            )
        )
        normals.append(jnp.sum(scaled_keys.astype(jnp.float32), axis=1))
        summary_sq.append(jnp.sum(carried * carried))
        summary_max.append(largest)
    open_flag = jnp.where(resets[width - 1] == 0, 1.0, 0.0).astype(jnp.float32).reshape(1)
    local_parts = (
        jnp.stack(sums, axis=1),
        jnp.stack(denoms, axis=1),
        jnp.stack(squares, axis=1),
        jnp.stack(maxima, axis=1),
        running.T,
        resets == 0,
        living,
    )
    summary = (
        jnp.stack(states),
        jnp.stack(normals),
        jnp.stack(summary_sq),
        jnp.stack(summary_max),
        running[:, width - 1],
        open_flag,
    )
    return (local_parts, summary)


def finish(local_parts, incoming, queries):
    sums, denoms, squares, maxima, running, first_open, living = local_parts
    state_in, normal_in, square_in, max_in = (incoming[0], incoming[1], incoming[2], incoming[3])
    incoming_exp = jnp.where(first_open[:, None], running + max_in[None, :], empty_max)
    largest = jnp.maximum(maxima, incoming_exp)
    own_scale = jnp.exp(maxima - largest)
    carry_scale = jnp.where(first_open[:, None], jnp.exp(incoming_exp - largest), 0.0)
    cross_term = jnp.einsum(
        "hdt,hdj->thj", queries, state_in.astype(jnp.bfloat16), preferred_element_type=jnp.float32
    )
    cross_den = jnp.einsum(
        "hdt,hd->th", queries, normal_in.astype(jnp.bfloat16), preferred_element_type=jnp.float32
    )
    numerator = own_scale[..., None] * sums + carry_scale[..., None] * cross_term
    denominator = own_scale * denoms + carry_scale * cross_den
    square = own_scale * own_scale * squares + carry_scale * carry_scale * square_in[None, :]
    divisor = jnp.where(living[:, None], jnp.maximum(jnp.abs(denominator), jnp.sqrt(square)), 1.0)
    result = jnp.where(living[:, None, None], numerator / divisor[..., None], 0.0)
    return result.reshape(result.shape[0], -1).astype(jnp.bfloat16)


def spread_prefix(summary):
    states, normals, sq_sum, top_sum, tails, open_flag = summary
    shards = lax.axis_size("seq")
    own_index = lax.axis_index("seq")
    head_count, key_dim, value_dim = states.shape
    row_count = head_count * key_dim // shards
    spread = lax.all_to_all(
        states.reshape(1, head_count * key_dim, value_dim),
        "seq",
        split_axis=1,
        concat_axis=0,
        tiled=True,
    )
    normal_all, square_all, top_all, tail_all, open_all = (
        lax.all_gather(normals[None], "seq", axis=0, tiled=True),
        lax.all_gather(sq_sum[None], "seq", axis=0, tiled=True),
        lax.all_gather(top_sum[None], "seq", axis=0, tiled=True),
        lax.all_gather(tails[None], "seq", axis=0, tiled=True),
        lax.all_gather(open_flag, "seq", axis=0, tiled=True),
    )
    tails_after = running_sum(tail_all.T).T
    before = tails_after - tail_all
    closed_after = running_sum(1.0 - open_all)
    closed_before = closed_after - (1.0 - open_all)
    shard_order = lax.iota(jnp.int32, shards)
    linked = (shard_order[:, None] < shard_order[None, :]) & (
        closed_before[None, :] - closed_after[:, None] < 0.5
    )
    exponent = top_all[:, None, :] + before[None, :, :] - tails_after[:, None, :]
    exponent = jnp.where(linked[..., None], exponent, empty_max)
    entry_max = jnp.max(exponent, axis=0)
    weight = jnp.where(linked[..., None], jnp.exp(exponent - entry_max[None]), 0.0)
    own_pick = (shard_order == own_index).astype(jnp.float32)
    own_weight = jnp.einsum("ijh,j->ih", weight, own_pick, precision=highest)
    normal_in = jnp.einsum("ih,ihd->hd", own_weight, normal_all, precision=highest)
    square_in = jnp.einsum("ih,ih->h", own_weight * own_weight, square_all, precision=highest)
    max_in = jnp.einsum("jh,j->h", entry_max, own_pick, precision=highest)
    row_head = (own_index * row_count + lax.iota(jnp.int32, row_count)) // key_dim
    head_pick = (lax.iota(jnp.int32, head_count)[:, None] == row_head[None, :]).astype(jnp.float32)
    row_weight = jnp.einsum("ijh,hr->jir", weight, head_pick, precision=highest)
    state_rows = jnp.einsum("jir,irc->jrc", row_weight, spread, precision=highest)
    returned = lax.all_to_all(
        state_rows.astype(jnp.bfloat16), "seq", split_axis=0, concat_axis=1, tiled=True
    ).astype(state_rows.dtype)
    return (returned.reshape(head_count, key_dim, value_dim), normal_in, square_in, max_in)


def body(qkv, igate, fgate, doc_start, lengths):
    regrouped = lax.all_to_all(qkv, "seq", split_axis=1, concat_axis=0, tiled=True)
    width = igate.shape[1]
    queries = regrouped[: HEAD_COUNT_HALF * DK].reshape(HEAD_COUNT_HALF, DK, width)
    key_rows = regrouped[HEAD_COUNT_HALF * DK : 2 * HEAD_COUNT_HALF * DK].reshape(
        HEAD_COUNT_HALF, DK, width
    )
    value_rows = regrouped[2 * HEAD_COUNT_HALF * DK :].reshape(HEAD_COUNT_HALF, DV, width)
    local_parts, summary = local_terms(
        queries, key_rows, value_rows, igate, fgate, doc_start, lengths[0]
    )
    incoming = spread_prefix(summary)
    return finish(local_parts, incoming, queries)


MESH = pl.DeviceIdType.MESH
f32, bf16 = jnp.float32, jnp.bfloat16
HEADS = HEAD_COUNT_HALF
PARTS = DV // 128


def dot_nt(a, b):
    return lax.dot_general(a, b, (((1,), (1,)), ((), ())), preferred_element_type=f32)


def worker_kernel(
    qkv, ig_hbm, fg_hbm, doc_hbm, live_len, out,
    ig, fg, doc, inbox, meta, metain, wts, qt, num, den, state, st_in, st_out, sm_in, sm_out, obuf,
    insend, inrecv, msend, mrecv, csend, crecv, osend, orecv, lsem,
):
    planes = HEADS
    width = ig_hbm.shape[1]
    span = planes * width
    g = lax.axis_index("groups")
    d = lax.axis_index("seq")
    p = lax.div(d, HEADS)
    h = lax.rem(d, HEADS)
    big = lax.div(d, 2 * HEADS)
    hd = (1 - big) * h + big * (lax.div(d, 2) - HEADS)
    role = (1 - big) * p + big * (2 + lax.rem(d, 2))
    peers = [lax.rem(h + i, HEADS) for i in range(1, HEADS)]

    loads = [
        pltpu.make_async_copy(src, dst, lsem.at[i])
        for i, (src, dst) in enumerate(((ig_hbm, ig), (fg_hbm, fg), (doc_hbm, doc)))
    ]
    for c in loads:
        c.start()

    bar = pltpu.get_barrier_semaphore()

    def greet(dev):
        pl.semaphore_signal(bar, inc=1, device_id=(g, dev), device_id_type=MESH)

    for s in (h, HEADS + h, 2 * HEADS + 2 * h, 2 * HEADS + 2 * h + 1):
        pl.when(s != d)(functools.partial(greet, s))
    for b in peers:
        greet(HEADS * p + b)
    pl.when(p > 0)(functools.partial(greet, d - HEADS))

    for c in loads:
        c.wait()
    pos = lax.broadcasted_iota(jnp.int32, (1, width), 1)
    live = pos < live_len[0]
    x = fg[...]
    a = jnp.where(live, jnp.minimum(x, 0.0) - jnp.log1p(jnp.exp(-jnp.abs(x))), 0.0)
    livef = jnp.where(live, 1.0, 0.0).astype(f32)
    docf = doc[...].astype(f32)
    pad = jnp.zeros((4, width), f32)
    for i in range(HEADS):
        meta[i] = jnp.concatenate([ig[i : i + 1, :], a[i : i + 1, :], docf, livef, pad], axis=0)

    count = 2 * HEADS - 1 + jnp.where(p < planes - 1, 1, 0) - jnp.where(hd == h, 1, 0)
    pl.semaphore_wait(bar, count)

    def remote(src, dst, ss, rs, dev):
        return pltpu.make_async_remote_copy(
            src_ref=src, dst_ref=dst, send_sem=ss, recv_sem=rs, device_id=(g, dev), device_id_type=MESH
        )

    mcopies = [
        remote(meta.at[b], metain.at[h], msend.at[i], mrecv.at[h], HEADS * p + b)
        for i, b in enumerate(peers)
    ]
    for c in mcopies:
        c.start()
    metain[h] = meta[h]

    def feature(j):
        return remote(
            qkv.at[:, pl.ds(j * span, span)], inbox.at[role], insend.at[j], inrecv.at[role], HEADS * j + hd
        )

    for j in range(planes):
        away = HEADS * j + hd != d

        @pl.when(away)
        def _():
            feature(j).start()

        @pl.when(jnp.logical_not(away))
        def _():
            pltpu.make_async_copy(
                qkv.at[:, pl.ds(j * span, span)], inbox.at[role], inrecv.at[role]
            ).start()

    def landed(slot):
        pltpu.make_async_copy(inbox.at[slot], inbox.at[slot], inrecv.at[slot]).wait()

    for i, b in enumerate(peers):
        pltpu.make_async_copy(metain.at[b], metain.at[b], mrecv.at[b]).wait()

    rows = jnp.concatenate([metain[b] for b in range(planes)], axis=1)
    ig_row, a_row, doc_row, live_row = (rows[i : i + 1, :] for i in range(4))
    ti = lax.broadcasted_iota(jnp.int32, (span, span), 0)
    si = lax.broadcasted_iota(jnp.int32, (span, span), 1)
    tri = ti >= si
    eye = ti == si
    b_col = jnp.sum(jnp.where(tri, a_row, 0.0), axis=1, keepdims=True)
    r_col = jnp.sum(jnp.where(tri, doc_row, 0.0), axis=1, keepdims=True)
    live_col = jnp.sum(jnp.where(eye, live_row, 0.0), axis=1, keepdims=True)
    b_row = jnp.sum(jnp.where(eye, b_col, 0.0), axis=0, keepdims=True)
    r_row = jnp.sum(jnp.where(eye, r_col, 0.0), axis=0, keepdims=True)
    allowed = tri & (r_col == r_row) & (live_row > 0.5)
    ex = jnp.where(allowed, b_col - b_row + ig_row, empty_max)
    top = jnp.max(ex, axis=1, keepdims=True)
    weights = jnp.where(allowed, jnp.exp(ex - top), 0.0)
    wts[...] = weights
    sq_own = jnp.sum(weights * weights, axis=1, keepdims=True)
    b_end = b_row[:, span - 1 : span]
    r_end = r_row[:, span - 1 : span]
    tail = (r_row == r_end) & (live_row > 0.5)
    cl = jnp.where(tail, b_end - b_row + ig_row, empty_max)
    mu = jnp.max(cl, axis=1, keepdims=True)
    u = jnp.where(tail, jnp.exp(cl - mu), 0.0)
    sq_sum = jnp.sum(u * u, axis=1, keepdims=True)
    key_scale = DK ** (-0.5)

    def own():
        landed(0)
        qt[...] = inbox[0].astype(f32).T.astype(bf16)
        for b in range(planes):
            r = pl.ds(b * width, width)
            score = jnp.dot(qt[r, :], inbox[1], preferred_element_type=f32) * key_scale
            w = wts[r, :] * score
            den[r, :] = jnp.sum(w, axis=1, keepdims=True)
            wb = w.astype(bf16)
            for f in range(2):
                num[r, pl.ds(f * DK, DK)] = dot_nt(wb, inbox[2 + f])

    @pl.when(p == 0)
    def _():
        st_in[...] = jnp.zeros(st_in.shape, bf16)
        sm_in[...] = jnp.concatenate(
            [jnp.zeros((16, DK), f32), jnp.full((8, DK), empty_max, f32)], axis=0
        )

    landed(1)
    keyw = (inbox[1].astype(f32) * (u * key_scale)).astype(bf16)
    n8 = dot_nt(jnp.ones((8, span), bf16), keyw)
    landed(2)
    landed(3)

    def product(c):
        return dot_nt(keyw, inbox[2 + c // 2, pl.ds((c % 2) * 128, 128), :])

    @pl.when((p > 0) & (p < planes - 1))
    def _():
        for c in range(PARTS):
            state[c] = product(c)

    pl.when(p >= 2)(own)

    sm_copy = remote(sm_out, sm_in, csend.at[PARTS], crecv.at[PARTS], d + HEADS)
    st_copies = [
        remote(st_out.at[c], st_in.at[c], csend.at[c], crecv.at[c], d + HEADS) for c in range(PARTS)
    ]

    @pl.when(p > 0)
    def _():
        pltpu.make_async_copy(sm_in, sm_in, crecv.at[PARTS]).wait()

    m_in = sm_in[16:17, 0:1]
    carried = b_end + m_in
    opened = r_end < 0.5
    largest = jnp.maximum(mu, jnp.where(opened, carried, empty_max))
    late = jnp.exp(mu - largest)
    early = jnp.where(opened, jnp.exp(carried - largest), 0.0)

    @pl.when(p < planes - 1)
    def _():
        sm_out[0:8, :] = late * n8 + early * sm_in[0:8, :]
        sm_out[8:16, :] = late * late * sq_sum + early * early * sm_in[8:16, :]
        sm_out[16:24, :] = jnp.broadcast_to(largest, (8, DK))
        sm_copy.start()

    for c in range(PARTS):

        @pl.when(p > 0)
        def _():
            pltpu.make_async_copy(st_in.at[c], st_in.at[c], crecv.at[c]).wait()

        @pl.when(p == 0)
        def _():
            st_out[c] = (late * product(c)).astype(bf16)
            st_copies[c].start()

        @pl.when((p > 0) & (p < planes - 1))
        def _():
            st_out[c] = (late * state[c] + early * st_in[c].astype(f32)).astype(bf16)
            st_copies[c].start()

    pl.when(p < 2)(own)

    nb = sm_in[0:8, :].astype(bf16)
    sq_in = sm_in[8:9, 0:1]

    def result(b):
        return remote(
            obuf.at[b], out.at[:, pl.ds(pl.multiple_of(h * DV, DV), DV)], osend.at[b], orecv.at[h], HEADS * p + b
        )

    def own_result(b):
        return pltpu.make_async_copy(
            obuf.at[b], out.at[:, pl.ds(pl.multiple_of(h * DV, DV), DV)], orecv.at[h]
        )

    for b in range(planes):
        lo, r = b * width, pl.ds(b * width, width)
        first = r_col[lo : lo + width] < 0.5
        f = jnp.where(first, b_col[lo : lo + width] + m_in, empty_max)
        mx = top[lo : lo + width]
        m = jnp.maximum(mx, f)
        xs = jnp.exp(mx - m)
        ys = jnp.where(first, jnp.exp(f - m), 0.0)
        qb = qt[r, :]
        dn = xs * den[r, :] + ys * dot_nt(qb, nb)[:, 0:1]
        sq = xs * xs * sq_own[lo : lo + width] + ys * ys * sq_in
        lv = live_col[lo : lo + width] > 0.5
        inv = 1.0 / jnp.where(lv, jnp.maximum(jnp.abs(dn), jnp.sqrt(sq)), 1.0)
        for c in range(PARTS):
            cs = pl.ds(c * 128, 128)
            cross = jnp.dot(qb, st_in[c], preferred_element_type=f32)
            obuf[b, :, cs] = jnp.where(lv, (xs * num[r, cs] + ys * cross) * inv, 0.0).astype(bf16)

        @pl.when(h != b)
        def _():
            result(b).start()

        @pl.when(h == b)
        def _():
            own_result(b).start()

    for i in range(HEADS):
        here = out.at[:, pl.ds(i * DV, DV)]
        pltpu.make_async_copy(here, here, orecv.at[i]).wait()
    for c in mcopies:
        c.wait_send()
    for j in range(planes):

        @pl.when(HEADS * j + hd != d)
        def _():
            feature(j).wait_send()

        @pl.when(h != j)
        def _():
            result(j).wait_send()

    @pl.when(p < planes - 1)
    def _():
        sm_copy.wait_send()
        for c in st_copies:
            c.wait_send()


def worker_body(qkv, igate, fgate, doc_start, lengths):
    width = igate.shape[1]
    span = HEADS * width
    anywhere = pl.BlockSpec(memory_space=pl.ANY)
    dma = pltpu.SemaphoreType.DMA
    return pl.pallas_call(
        worker_kernel,
        out_shape=jax.ShapeDtypeStruct((width, HEADS * DV), bf16),
        in_specs=[anywhere] * 4 + [pl.BlockSpec(memory_space=pltpu.SMEM)],
        out_specs=pl.BlockSpec(memory_space=pl.ANY),
        scratch_shapes=[
            pltpu.VMEM((HEADS, width), f32),
            pltpu.VMEM((HEADS, width), f32),
            pltpu.VMEM((1, width), jnp.int32),
            pltpu.VMEM((4, DK, span), bf16),
            pltpu.VMEM((HEADS, 8, width), f32),
            pltpu.VMEM((HEADS, 8, width), f32),
            pltpu.VMEM((span, span), f32),
            pltpu.VMEM((span, DK), bf16),
            pltpu.VMEM((span, DV), f32),
            pltpu.VMEM((span, 1), f32),
            pltpu.VMEM((PARTS, DK, 128), f32),
            pltpu.VMEM((PARTS, DK, 128), bf16),
            pltpu.VMEM((PARTS, DK, 128), bf16),
            pltpu.VMEM((24, DK), f32),
            pltpu.VMEM((24, DK), f32),
            pltpu.VMEM((HEADS, width, DV), bf16),
            dma((HEADS,)), dma((4,)), dma((HEADS - 1,)), dma((HEADS,)),
            dma((PARTS + 1,)), dma((PARTS + 1,)), dma((HEADS,)), dma((HEADS,)), dma((3,)),
        ],
        compiler_params=pltpu.CompilerParams(
            collective_id=0, has_side_effects=True, vmem_limit_bytes=60 * 1024 * 1024
        ),
    )(qkv, igate, fgate, doc_start.reshape(1, width), lengths)


def solution(mesh):
    placed = (
        P("seq", "groups"),
        P(None, ("groups", "seq")),
        P(None, ("groups", "seq")),
        P(("groups", "seq")),
        P(("groups", "seq")),
    )
    shards = mesh.shape["seq"]
    whole_heads = shards == HEADS * HEADS and shards * DK == 2 * HEADS * DK + HEADS * DV
    return jax.shard_map(
        worker_body if whole_heads else body, mesh=mesh, in_specs=placed, out_specs=P(("groups", "seq"), None), check_vma=False
    )
```
